32 devices in a mesh: wide: 16 (over z, x, core), hub: 2 (over y).
Axes of the slice: x: 2, y: 2, z: 4, core: 2. Of those that a mesh axis runs over, the one named last changes fastest.
Arguments:
- low_feats: bfloat16 [8192, 256], P(('wide', 'hub')), may hold values from -6 to 6
- hub_feats: bfloat16 [512, 256], P(('wide', 'hub')), may hold values from -6 to 6
- w_first: bfloat16 [256, 256], replicated, may hold values from -0.375 to 0.375
- w_second: bfloat16 [256, 256], replicated, may hold values from -0.375 to 0.375
- low_tiles: bfloat16 [1024, 128, 128], P(('wide', 'hub')), may hold values from 0 to 1.5
- tile_cols: int32 [64, 16], P(('wide', 'hub')), may hold values from 0 to 31, all different within a row
- edge_rows: int32 [16384], P(('wide', 'hub')), may hold values from 0 to 255
- edge_hubs: int32 [16384], P(('wide', 'hub')), may hold values from 0 to 31
- low_labels: int32 [8192], P(('wide', 'hub')), may hold values from 0 to 255
- hub_labels: int32 [512], P(('wide', 'hub')), may hold values from 0 to 255
Outputs:
- low_logits: float32 [8192, 256], P(('wide', 'hub'))
- hub_logits: float32 [512, 256], P(('wide', 'hub'))
- grad_first: float32 [256, 256], replicated
- grad_second: float32 [256, 256], replicated
The draws below stay inside these ranges and needn't reach their ends.
Inputs may be any that keep to these rules, and one draw needn't show every extreme that they name: `tile_cols`: the 16 tiles of one row block have different column blocks.
All inputs are finite; a program needn't handle non-finite values.
Results may differ from the reference program's by a relative error of at most 0.0022.
The reference program's roundings to bfloat16 on the way count: a program that leaves them out, or rounds other values in their place, can miss the bound.
Values may be sent and summed in bfloat16 or wider, within the bound.
No kernel may reach another device: no remote copies, remote signals or barrier semaphores. Data moves between devices by JAX's collectives and lax.ppermute only.
A program may use at most 64 MiB of HBM per device.

```python
import math
import jax
import jax.numpy as jnp
import numpy as np
from jax import lax

FEAT = 256
UNITS = 256
CLASSES = 256
TILE = 128
TILES_ROW = 16
BLOCKS_DEV = 2
ROWS_DEV = 256
EDGES_DEV = 512
GROUP_BLOCKS = 32
HUBS_GRP = 32
VERTS = 8192
HUBS = 512
TOTAL = 8704
N_WIDE = 16
N_HUB = 2


def draw_low_tiles(key, part):
    shape = (N_WIDE * N_HUB * BLOCKS_DEV * TILES_ROW, TILE, TILE)
    keep_key, value_key = jax.random.split(key)
    keep = jax.random.bernoulli(keep_key, 0.0625, shape)
    values = jax.random.uniform(value_key, shape, jnp.float32, 0.5, 1.5)
    return jnp.where(keep, values, 0.0).astype(jnp.bfloat16)


def touch_ends(entries, own_key, least, high):
    longest = entries.shape.index(max(entries.shape))
    spots = []
    for shift in (0, 1):
        where = [jax.random.randint(jax.random.fold_in(own_key, axis), (), 0, length) for axis, length in enumerate(entries.shape)]
        where[longest] = (where[longest] + shift) % entries.shape[longest]
        spots.append(tuple(where))
    return entries.at[spots[0]].set(least).at[spots[1]].set(high)


def level_of(own_key, extent, cuts, low, top_value):
    factor_of = 1.0
    for axis_at, shards_of in cuts:
        draws = jax.random.uniform(jax.random.fold_in(jax.random.fold_in(own_key, 6), axis_at), (shards_of,), jnp.float32, low / len(cuts), top_value / len(cuts))
        factor_of = factor_of * jnp.repeat(jnp.exp(draws), extent[axis_at] // shards_of).reshape((-1,) + (1,) * (len(extent) - 1 - axis_at))
    return factor_of


def cumulative_ranks(number_of, skew):
    loads = [(1 << 20) // math.isqrt(rank ** skew) + 1 for rank in range(1, number_of + 1)]
    scale = 1 + sum(loads) // (1 << 30)
    return np.cumsum(np.array([max(1, weight // scale) for weight in loads]))


def skewed_ids(own_key, shape, count, slope):
    table = cumulative_ranks(count, slope)
    lot = jax.random.randint(jax.random.fold_in(own_key, 1), shape, 0, int(table[count - 1]))
    rank = jnp.searchsorted(jnp.asarray(table, jnp.int32), lot, side="right")
    return jax.random.permutation(jax.random.fold_in(own_key, 2), count)[rank].astype(jnp.int32)


def distinct(own_key, rows, amount, top, lift):
    order = jax.random.permutation(jax.random.fold_in(own_key, 1), amount)
    pull = order
    for power in range(3):
        pull = pull * pull // amount
    pull = pull * lift // amount
    tickets = jax.random.randint(jax.random.fold_in(own_key, 2), (rows, amount), 0, 4096) + pull
    fixed_rows = jax.random.permutation(jax.random.fold_in(own_key, 3), rows)[jnp.arange(amount) % rows]
    tickets = jnp.where(jnp.arange(rows)[:, None] == fixed_rows[None, :], 1 << 14, tickets)
    priority = tickets * amount + jnp.arange(amount)
    return lax.top_k(priority.astype(jnp.int32), top)[1].astype(jnp.int32)


def centred(own_key, shape, deviation, reach, pieces=(), kind=jnp.bfloat16):
    entries = deviation * jax.random.normal(own_key, shape, jnp.float32)
    if pieces:
        entries = entries * level_of(own_key, shape, pieces, -0.22, 0.18)
    return jnp.clip(entries, -reach, reach).astype(kind)


def setup_inputs(seed: int = 0) -> dict:
    key_of = jax.random.split(jax.random.key(seed), 11)
    low_feats = centred(key_of[0], (VERTS, FEAT), 1.0, 6.0, ((0, 32),))
    hub_feats = centred(key_of[1], (HUBS, FEAT), 1.0, 6.0, ((0, 32),))
    w_first = centred(key_of[2], (FEAT, UNITS), FEAT ** -0.5, 0.375)
    w_second = centred(key_of[3], (UNITS, CLASSES), UNITS ** -0.5, 0.375)
    low_tiles = draw_low_tiles(jax.random.fold_in(key_of[10], 71), 0)
    tile_cols = distinct(key_of[5], (VERTS // TILE), GROUP_BLOCKS, TILES_ROW, 0)
    edge_rows = touch_ends(jax.random.randint(key_of[6], (N_WIDE * N_HUB * EDGES_DEV,), 0, ROWS_DEV), jax.random.fold_in(key_of[6], 1), 0, ROWS_DEV - 1).astype(jnp.int32)
    edge_hubs = touch_ends(skewed_ids(key_of[7], (N_WIDE * N_HUB * EDGES_DEV,), HUBS_GRP, 2), jax.random.fold_in(key_of[7], 3), 0, HUBS_GRP - 1).astype(jnp.int32)
    low_labels = touch_ends(jax.random.randint(key_of[8], (VERTS,), 0, CLASSES), jax.random.fold_in(key_of[8], 1), 0, CLASSES - 1).astype(jnp.int32)
    hub_labels = touch_ends(jax.random.randint(key_of[9], (HUBS,), 0, CLASSES), jax.random.fold_in(key_of[9], 1), 0, CLASSES - 1).astype(jnp.int32)
    return dict(low_feats=low_feats, hub_feats=hub_feats, w_first=w_first, w_second=w_second, low_tiles=low_tiles, tile_cols=tile_cols, edge_rows=edge_rows, edge_hubs=edge_hubs, low_labels=low_labels, hub_labels=hub_labels)


def graph_tables(low_tiles, edge_rows, edge_hubs):
    edge_total = N_WIDE * N_HUB * EDGES_DEV
    device_of = jnp.arange(edge_total, dtype=jnp.int32) // EDGES_DEV
    low_index = (device_of * ROWS_DEV + edge_rows).astype(jnp.int32)
    hub_index = (device_of // N_HUB * HUBS_GRP + edge_hubs).astype(jnp.int32)
    ones = jnp.ones((edge_total,), jnp.float32)
    low_count = jax.ops.segment_sum(ones, low_index, VERTS)
    hub_count = jax.ops.segment_sum(ones, hub_index, HUBS)
    tile_rows = lax.optimization_barrier(jnp.sum(low_tiles.astype(jnp.float32), axis=2))
    tile_rows = lax.optimization_barrier(jnp.sum(tile_rows.reshape(VERTS // TILE, TILES_ROW, TILE), axis=1)).reshape(VERTS)
    low_scale = lax.rsqrt(1.0 + tile_rows + low_count)
    hub_scale = lax.rsqrt(1.0 + hub_count)
    return (low_index, hub_index, low_scale, hub_scale)

def tiles_forward(field_low, low_tiles, tile_cols):
    width = field_low.shape[1]
    grid = field_low.astype(jnp.float32).reshape(N_WIDE, N_HUB, BLOCKS_DEV, TILE, width)
    by_group = jnp.transpose(grid, (1, 0, 2, 3, 4)).reshape(N_HUB, N_WIDE * BLOCKS_DEV, TILE, width)
    tiles = low_tiles.reshape(N_WIDE, N_HUB, BLOCKS_DEV, TILES_ROW, TILE, TILE)
    cols = tile_cols.reshape(N_WIDE, N_HUB, BLOCKS_DEV, TILES_ROW)
    hub_ids = jnp.arange(N_HUB, dtype=jnp.int32)[:, None, None]

    def one_wide(wide_index):
        picked = by_group[hub_ids, cols[wide_index]]
        return jnp.einsum('hrkij,hrkjf->hrif', tiles[wide_index].astype(jnp.float32), picked)
    result = lax.map(one_wide, jnp.arange(N_WIDE, dtype=jnp.int32))
    return result.reshape(VERTS, width)

def tiles_backward(q_low, low_tiles, tile_cols):
    width = q_low.shape[1]
    grid = q_low.astype(jnp.float32).reshape(N_WIDE, N_HUB, BLOCKS_DEV, TILE, width)
    tiles = low_tiles.reshape(N_WIDE, N_HUB, BLOCKS_DEV, TILES_ROW, TILE, TILE)
    cols = tile_cols.reshape(N_WIDE, N_HUB, BLOCKS_DEV, TILES_ROW)
    hub_ids = jnp.arange(N_HUB, dtype=jnp.int32)[:, None, None]

    def step(total, wide_index):
        contrib = jnp.einsum('hrkij,hrif->hrkjf', tiles[wide_index].astype(jnp.float32), grid[wide_index])
        return (total.at[hub_ids, cols[wide_index]].add(contrib), None)
    start = jnp.zeros((N_HUB, N_WIDE * BLOCKS_DEV, TILE, width), jnp.float32)
    total, _ = lax.scan(step, start, jnp.arange(N_WIDE, dtype=jnp.int32))
    total = total.reshape(N_HUB, N_WIDE, BLOCKS_DEV, TILE, width)
    return jnp.transpose(total, (1, 0, 2, 3, 4)).reshape(VERTS, width)

def edge_sums(field_low, field_hub, low_index, hub_index):
    to_low = jax.ops.segment_sum(field_hub.astype(jnp.float32)[hub_index], low_index, VERTS)
    to_hub = jax.ops.segment_sum(field_low.astype(jnp.float32)[low_index], hub_index, HUBS)
    return (to_low, to_hub)

def reference(low_feats, hub_feats, w_first, w_second, low_tiles, tile_cols, edge_rows, edge_hubs, low_labels, hub_labels):
    low_index, hub_index, low_scale, hub_scale = graph_tables(low_tiles, edge_rows, edge_hubs)

    def propagate(field_low, field_hub):
        to_low, to_hub = edge_sums(field_low, field_hub, low_index, hub_index)
        out_low = (field_low.astype(jnp.float32) + tiles_forward(field_low, low_tiles, tile_cols) + to_low) * low_scale[:, None]
        out_hub = (field_hub.astype(jnp.float32) + to_hub) * hub_scale[:, None]
        return (out_low.astype(jnp.bfloat16), out_hub.astype(jnp.bfloat16))
    agg1_low, agg1_hub = propagate(low_feats, hub_feats)
    z1_low = jnp.dot(agg1_low, w_first, preferred_element_type=jnp.float32)
    z1_hub = jnp.dot(agg1_hub, w_first, preferred_element_type=jnp.float32)
    h1_low = jnp.maximum(z1_low, 0.0).astype(jnp.bfloat16)
    h1_hub = jnp.maximum(z1_hub, 0.0).astype(jnp.bfloat16)
    agg2_low, agg2_hub = propagate(h1_low, h1_hub)
    low_logits = jnp.dot(agg2_low, w_second, preferred_element_type=jnp.float32)
    hub_logits = jnp.dot(agg2_hub, w_second, preferred_element_type=jnp.float32)
    classes = jnp.arange(CLASSES, dtype=jnp.int32)
    low_target = (low_labels[:, None] == classes[None, :]).astype(jnp.float32)
    hub_target = (hub_labels[:, None] == classes[None, :]).astype(jnp.float32)
    dz2_low = ((low_logits - low_target) / TOTAL).astype(jnp.bfloat16)
    dz2_hub = ((hub_logits - hub_target) / TOTAL).astype(jnp.bfloat16)
    grad_second = jnp.dot(agg2_low.T, dz2_low, preferred_element_type=jnp.float32) + jnp.dot(agg2_hub.T, dz2_hub, preferred_element_type=jnp.float32)
    q_low = (jnp.dot(dz2_low, w_second.T, preferred_element_type=jnp.float32) * low_scale[:, None]).astype(jnp.bfloat16)
    q_hub = (jnp.dot(dz2_hub, w_second.T, preferred_element_type=jnp.float32) * hub_scale[:, None]).astype(jnp.bfloat16)
    to_low, to_hub = edge_sums(q_low, q_hub, low_index, hub_index)
    dh1_low = q_low.astype(jnp.float32) + tiles_backward(q_low, low_tiles, tile_cols) + to_low
    dh1_hub = q_hub.astype(jnp.float32) + to_hub
    dz1_low = jnp.where(z1_low > 0.0, dh1_low, 0.0).astype(jnp.bfloat16)
    dz1_hub = jnp.where(z1_hub > 0.0, dh1_hub, 0.0).astype(jnp.bfloat16)
    grad_first = jnp.dot(agg1_low.T, dz1_low, preferred_element_type=jnp.float32) + jnp.dot(agg1_hub.T, dz1_hub, preferred_element_type=jnp.float32)
    return (low_logits, hub_logits, grad_first, grad_second)
```

```python
import jax
import jax.numpy as jnp
from jax import lax
from jax.experimental import pallas as pl
from jax.experimental.pallas import tpu as pltpu
from jax.sharding import PartitionSpec as P

F32 = jnp.float32
BF16 = jnp.bfloat16
WIDE = "wide"
HUB = "hub"
LANES = 128


def shaped(rows, cols, dtype):
    return jax.ShapeDtypeStruct((rows, cols), dtype)


def call(body, name, outs, ins, smem=(), scratch=()):
    spaces = [pltpu.SMEM if i in smem else pltpu.VMEM for i in range(len(ins))]
    return pl.pallas_call(
        body,
        name=name,
        out_shape=outs,
        in_specs=[pl.BlockSpec(memory_space=s) for s in spaces],
        out_specs=[pl.BlockSpec(memory_space=pltpu.VMEM) for _ in outs],
        scratch_shapes=list(scratch),
        compiler_params=pltpu.CompilerParams(vmem_limit_bytes=28 * 1024 * 1024),
    )(*ins)


def dot(a, b):
    return lax.dot_general(a, b, (((1,), (0,)), ((), ())), preferred_element_type=F32)


def dot_nt(a, b):
    return lax.dot_general(a, b, (((1,), (1,)), ((), ())), preferred_element_type=F32)


def dot_tn(a, b):
    return lax.dot_general(a, b, (((0,), (0,)), ((), ())), preferred_element_type=F32)


def to_wide(x, k):
    return lax.ppermute(x, WIDE, [(i, i ^ k) for i in range(lax.axis_size(WIDE))])


def to_both(x, k, j):
    n, m = lax.axis_size(WIDE), lax.axis_size(HUB)
    pairs = [(i * m + h, (i ^ k) * m + (h ^ j)) for i in range(n) for h in range(m)]
    return lax.ppermute(x, (WIDE, HUB), pairs)


def gather_wide(first, second):
    nz = lax.axis_size(WIDE) // 4
    xb = to_wide(second, 2)
    za = [to_wide(first, 4 * k) for k in range(1, nz)]
    b2 = jnp.concatenate([second, xb], axis=0)
    a4 = jnp.concatenate([first] + za, axis=0)
    xa = to_wide(a4, 2)
    zb = [to_wide(b2, 4 * k) for k in range(1, nz)]
    near = [a4, xa, b2] + zb
    return near + [to_wide(p, 1) for p in near]


def pairwise(parts):
    while len(parts) > 1:
        parts = [parts[i] + parts[i + 1] for i in range(0, len(parts), 2)]
    return parts[0]


def tile_sum(adj_ref, piece_refs):
    at, total = 0, None
    for ref in piece_refs:
        n = ref.shape[0]
        term = dot(adj_ref[:, at : at + n], ref[...])
        total = term if total is None else total + term
        at += n
    return total


def local(
    low_feats,
    hub_feats,
    w_first,
    w_second,
    low_tiles,
    tile_cols,
    edge_rows,
    edge_hubs,
    low_labels,
    hub_labels,
):
    rows, feat = low_feats.shape
    hr = hub_feats.shape[0]
    n_tiles, tile, _ = low_tiles.shape
    blocks = rows // tile
    per_block = n_tiles // blocks
    units = w_first.shape[1]
    classes = w_second.shape[1]
    n_wide, n_hub = lax.axis_size(WIDE), lax.axis_size(HUB)
    nz = n_wide // 4
    group = hr * n_hub
    total = (rows + hr) * n_wide * n_hub
    edges = edge_rows.shape[0]
    half = n_wide * rows // 2
    pay = feat + LANES

    def prep(tiles, cols, e_rows, e_hubs, feats, adj, adj_t, adj_t_give, link, link_t, scale, *parts):
        w, h = lax.axis_index(WIDE), lax.axis_index(HUB)
        adj[...] = jnp.zeros_like(adj)
        adj_t[...] = jnp.zeros_like(adj_t)
        adj_t_give[...] = jnp.zeros_like(adj_t_give)
        for r in range(blocks):
            for k in range(per_block):
                b = cols[r, k]
                rel = (b // 2) ^ w
                rc, rx, rz = rel & 1, (rel >> 1) & 1, rel >> 2
                place = jnp.where(b % 2 == 0, rx * nz + rz, 2 * nz + rz * 2 + rx)
                start = pl.multiple_of(place * tile, tile)
                value = tiles[r * per_block + k]
                turned = value.T
                adj[r * tile : (r + 1) * tile, pl.ds(pl.multiple_of(rc * half + start, tile), tile)] = value

                @pl.when(rc == 0)
                def _():
                    adj_t[pl.ds(start, tile), r * tile : (r + 1) * tile] = turned

                @pl.when(rc == 1)
                def _():
                    adj_t_give[pl.ds(start, tile), r * tile : (r + 1) * tile] = turned

        hubs = e_hubs[...]
        hubs = ((hubs // hr) ^ h) * hr + hubs % hr
        row_hot = (lax.broadcasted_iota(jnp.int32, (rows, edges), 0) == e_rows[...]).astype(BF16)
        hub_hot = (lax.broadcasted_iota(jnp.int32, (group, edges), 0) == hubs).astype(BF16)
        links = dot_nt(hub_hot, row_hot)
        links_t = dot_nt(row_hot, hub_hot)
        hi, hi_t = links.astype(BF16), links_t.astype(BF16)
        lo, lo_t = (links - hi.astype(F32)).astype(BF16), (links_t - hi_t.astype(F32)).astype(BF16)
        link[:, :rows] = hi
        link[:, rows:] = lo
        link_t[...] = jnp.concatenate([hi_t, lo_t], axis=1)
        deg = dot(adj[...], jnp.ones((2 * half, LANES), BF16))
        deg = 1.0 + deg + jnp.sum(links_t, axis=1, keepdims=True)
        scale[...] = lax.rsqrt(deg)
        sums = dot(hi, feats[...]) + dot(lo, feats[...])
        counts = jnp.broadcast_to(jnp.sum(links, axis=1, keepdims=True), (group, LANES))
        for k, part in enumerate(parts):
            part[:, :feat] = sums[k * hr : (k + 1) * hr]
            part[:, feat:] = counts[k * hr : (k + 1) * hr]

    adj, adj_t, adj_t_give, link, link_t, scale, *parts1 = call(
        prep,
        "prep",
        [
            shaped(rows, 2 * half, BF16),
            shaped(half, rows, BF16),
            shaped(half, rows, BF16),
            shaped(group, 2 * rows, BF16),
            shaped(rows, 2 * group, BF16),
            shaped(rows, LANES, F32),
        ]
        + [shaped(hr, pay, F32) for _ in range(n_hub)],
        [low_tiles, tile_cols, edge_rows.reshape(1, edges), edge_hubs.reshape(1, edges), low_feats],
        smem=(1,),
    )
    adj_t_mate = to_wide(adj_t_give, 1)

    def to_hub(x, k):
        return lax.ppermute(x, HUB, [(i, i ^ k) for i in range(n_hub)])

    mates = range(1, n_hub)
    feats_mates = [to_hub(hub_feats, k) for k in mates]
    got1 = [to_hub(parts1[k], k) for k in mates]

    def hub_first(feats, w, own, *refs):
        got, (hub_scale, agg, act, live) = refs[:-4], refs[-4:]
        sums = own[...]
        for g in got:
            sums = sums + g[...]
        s = lax.rsqrt(1.0 + sums[:, feat : feat + 1])
        hub_scale[...] = jnp.broadcast_to(s, (hr, LANES))
        a = ((feats[...].astype(F32) + sums[:, :feat]) * s).astype(BF16)
        agg[...] = a
        z = dot(a, w[...])
        act[...] = jnp.maximum(z, 0.0).astype(BF16)
        live[...] = (z > 0.0).astype(F32)

    hub_scale, agg1_hub, h1_hub, live_hub = call(
        hub_first,
        "hub_first",
        [shaped(hr, LANES, F32), shaped(hr, feat, BF16), shaped(hr, units, BF16), shaped(hr, units, F32)],
        [hub_feats, w_first, parts1[0]] + got1,
    )

    first, second = low_feats[:tile], low_feats[tile:]
    pieces1 = gather_wide(first, second)
    n_pieces = len(pieces1)

    def low_first(adj, link, link_t, scale, field, w, act_hub, *refs):
        pieces, refs = refs[:n_pieces], refs[n_pieces:]
        hubs, refs = refs[:n_hub], refs[n_hub:]
        agg, act_a, act_b, live, own, *sends = refs
        around = jnp.concatenate([r[...] for r in hubs] * 2, axis=0)
        s = tile_sum(adj, pieces) + field[...].astype(F32) + dot(link_t[...], around)
        a = (s * scale[:, :1]).astype(BF16)
        agg[...] = a
        z = dot(a, w[...])
        act = jnp.maximum(z, 0.0).astype(BF16)
        act_a[...] = act[:tile]
        act_b[...] = act[tile:]
        live[...] = (z > 0.0).astype(BF16)
        sums = dot(link[:, :rows], act) + dot(link[:, rows:], act)
        own[...] = sums[:hr]
        for k, send in enumerate(sends, 1):
            send[:hr] = act_hub[...].astype(F32)
            send[hr:] = sums[k * hr : (k + 1) * hr]

    agg1, h1_a, h1_b, live, own2, *sends2 = call(
        low_first,
        "low_first",
        [
            shaped(rows, feat, BF16),
            shaped(tile, units, BF16),
            shaped(rows - tile, units, BF16),
            shaped(rows, units, BF16),
            shaped(hr, units, F32),
        ]
        + [shaped(2 * hr, units, F32) for _ in mates],
        [adj, link, link_t, scale, low_feats, w_first, h1_hub] + pieces1 + [hub_feats] + feats_mates,
    )
    pieces2 = gather_wide(h1_a, h1_b)
    got2 = [to_hub(x, k) for k, x in enumerate(sends2, 1)]

    def hub_second(act, hub_scale, w, labels, own, *refs):
        got, (logits, agg, dz, q) = refs[:-4], refs[-4:]
        sums = own[...]
        for g in got:
            sums = sums + g[hr:]
        s = hub_scale[:, :1]
        a = ((act[...].astype(F32) + sums) * s).astype(BF16)
        agg[...] = a
        y = dot(a, w[...])
        logits[...] = y
        target = (lax.broadcasted_iota(jnp.int32, (hr, classes), 1) == labels[...]).astype(F32)
        d = ((y - target) / total).astype(BF16)
        dz[...] = d
        q[...] = (dot_nt(d, w[...]) * s).astype(BF16)

    hub_logits, agg2_hub, dz2_hub, q_hub = call(
        hub_second,
        "hub_second",
        [shaped(hr, classes, F32), shaped(hr, units, BF16), shaped(hr, classes, BF16), shaped(hr, units, BF16)],
        [h1_hub, hub_scale, w_second, hub_labels.reshape(hr, 1), own2] + got2,
    )

    def low_second(adj, link, link_t, scale, act_a, act_b, w, labels, act_hub, agg_hub, dz_hub, q_hub, *refs):
        pieces, refs = refs[:n_pieces], refs[n_pieces:]
        got, refs = refs[: n_hub - 1], refs[n_hub - 1 :]
        logits, grad, q_out, own, *sends = refs
        around = jnp.concatenate([act_hub[...]] + [g[:hr].astype(BF16) for g in got], axis=0)
        around = jnp.concatenate([around, around], axis=0)
        field = jnp.concatenate([act_a[...], act_b[...]], axis=0).astype(F32)
        s = tile_sum(adj, pieces) + field + dot(link_t[...], around)
        a = (s * scale[:, :1]).astype(BF16)
        y = dot(a, w[...])
        logits[...] = y
        target = (lax.broadcasted_iota(jnp.int32, (rows, classes), 1) == labels[...]).astype(F32)
        d = ((y - target) / total).astype(BF16)
        q = (dot_nt(d, w[...]) * scale[:, :1]).astype(BF16)
        q_out[...] = q
        grad[...] = dot_tn(a, d) + dot_tn(agg_hub[...], dz_hub[...])
        sums = dot(link[:, :rows], q) + dot(link[:, rows:], q)
        own[...] = sums[:hr]
        for k, send in enumerate(sends, 1):
            send[:hr] = q_hub[...].astype(F32)
            send[hr:] = sums[k * hr : (k + 1) * hr]

    low_logits, grad_second, q_low, own3, *sends3 = call(
        low_second,
        "low_second",
        [shaped(rows, classes, F32), shaped(units, classes, F32), shaped(rows, units, BF16), shaped(hr, units, F32)]
        + [shaped(2 * hr, units, F32) for _ in mates],
        [adj, link, link_t, scale, h1_a, h1_b, w_second, low_labels.reshape(rows, 1), h1_hub, agg2_hub, dz2_hub, q_hub]
        + pieces2
        + got2,
    )
    q_mate = to_wide(q_low, 1)
    got3 = [to_hub(x, k) for k, x in enumerate(sends3, 1)]

    quarter = nz * tile

    def transposed(adj_t, adj_t_mate, q, q_mate, keep_a, keep_b, send_x, *sends_z):
        def terms(at, n):
            return dot(adj_t[at : at + n], q[...]) + dot(adj_t_mate[at : at + n], q_mate[...])

        send_x[...] = terms(quarter, quarter).astype(BF16)
        for k, send in enumerate(sends_z, 1):
            send[...] = terms(2 * quarter + 2 * k * tile, 2 * tile).astype(BF16)
        keep_a[...] = terms(0, quarter)
        keep_b[...] = terms(2 * quarter, 2 * tile)

    keep_a, keep_b, send_x, *sends_z = call(
        transposed,
        "transposed",
        [shaped(quarter, units, F32), shaped(2 * tile, units, F32), shaped(quarter, units, BF16)]
        + [shaped(2 * tile, units, BF16) for _ in range(1, nz)],
        [adj_t, adj_t_mate, q_low, q_mate],
    )
    got_x = to_wide(send_x, 2)
    gots_z = [to_wide(x, 4 * k) for k, x in enumerate(sends_z, 1)]

    def sum_x(keep, got, own, *sends):
        own[...] = keep[:tile] + got[:tile].astype(F32)
        for k, send in enumerate(sends, 1):
            at = slice(k * tile, (k + 1) * tile)
            send[...] = (keep[at] + got[at].astype(F32)).astype(BF16)

    own_a, *sends_a = call(
        sum_x,
        "sum_x",
        [shaped(tile, units, F32)] + [shaped(tile, units, BF16) for _ in range(1, nz)],
        [keep_a, got_x],
    )
    gots_a = [to_wide(x, 4 * k) for k, x in enumerate(sends_a, 1)]

    def sum_z(keep, *refs):
        gots, (own, send) = refs[:-2], refs[-2:]
        s = keep[...]
        for g in gots:
            s = s + g[...].astype(F32)
        own[...] = s[:tile]
        send[...] = s[tile:].astype(BF16)

    own_b, send_b = call(sum_z, "sum_z", [shaped(tile, units, F32), shaped(tile, units, BF16)], [keep_b] + gots_z)
    got_b = to_wide(send_b, 2)

    def back_first(own_a, own_b, got_b, q, live, link_t, agg, agg_hub, q_hub, live_hub, own3, grad_second, *refs):
        gots_a, refs = refs[: nz - 1], refs[nz - 1 :]
        got3, (keep, give) = refs[: n_hub - 1], refs[n_hub - 1 :]
        back_a = own_a[...]
        for g in gots_a:
            back_a = back_a + g[...].astype(F32)
        back_b = own_b[...] + got_b[...].astype(F32)
        around = jnp.concatenate([q_hub[...]] + [g[:hr].astype(BF16) for g in got3], axis=0)
        around = jnp.concatenate([around, around], axis=0)
        dh = q[...].astype(F32) + jnp.concatenate([back_a, back_b], axis=0) + dot(link_t[...], around)
        dz = jnp.where(live[...].astype(F32) > 0.0, dh, 0.0).astype(BF16)
        sums = own3[...]
        for g in got3:
            sums = sums + g[hr:]
        dh_hub = q_hub[...].astype(F32) + sums
        dz_hub = jnp.where(live_hub[...] > 0.0, dh_hub, 0.0).astype(BF16)
        grad = dot_tn(agg[...], dz) + dot_tn(agg_hub[...], dz_hub)
        core = lax.axis_index(WIDE) & 1

        @pl.when(core == 0)
        def _():
            keep[...] = grad
            give[...] = grad_second[...]

        @pl.when(core == 1)
        def _():
            keep[...] = grad_second[...]
            give[...] = grad

    keep, give = call(
        back_first,
        "back_first",
        [shaped(units, classes, F32), shaped(units, classes, F32)],
        [own_a, own_b, got_b, q_low, live, link_t, agg1, agg1_hub, q_hub, live_hub, own3, grad_second] + gots_a + got3,
    )
    got = to_wide(give, 1)

    n_share = 2 * n_hub
    share = units // n_share
    steps = [(2 * (k // n_hub), k % n_hub) for k in range(n_share)]

    def place_of():
        return ((lax.axis_index(WIDE) >> 1) & 1) * n_hub + lax.axis_index(HUB)

    def split(keep, got, *outs):
        me = place_of()
        for k, out in enumerate(outs):
            at = pl.ds(pl.multiple_of((me ^ k) * share, share), share)
            out[...] = keep[at] + got[at]

    shares = call(split, "split", [shaped(share, classes, F32) for _ in range(n_share)], [keep, got])
    shares = [shares[0]] + [to_both(shares[k], *steps[k]) for k in range(1, n_share)]

    def add_up(*refs):
        refs[-1][...] = pairwise([r[...] for r in refs[:-1]])

    (mine,) = call(add_up, "add_xy", [shaped(share, classes, F32)], shares)
    (mine,) = call(
        add_up, "add_z", [shaped(share, classes, F32)], [mine] + [to_wide(mine, 4 * k) for k in range(1, nz)]
    )
    mine = [mine] + [to_both(mine, *steps[k]) for k in range(1, n_share)]
    other = [to_wide(m, 1) for m in mine]

    def assemble(*refs):
        mine, other, (grad_first, grad_second) = refs[:n_share], refs[n_share : 2 * n_share], refs[2 * n_share :]
        me = place_of()
        core = lax.axis_index(WIDE) & 1

        def write(mine_out, other_out):
            for k in range(n_share):
                at = pl.ds(pl.multiple_of((me ^ k) * share, share), share)
                mine_out[at] = mine[k][...]
                other_out[at] = other[k][...]

        @pl.when(core == 0)
        def _():
            write(grad_first, grad_second)

        @pl.when(core == 1)
        def _():
            write(grad_second, grad_first)

    grad_first, grad_second = call(
        assemble, "assemble", [shaped(units, classes, F32), shaped(units, classes, F32)], mine + other
    )
    return (low_logits, hub_logits, grad_first, grad_second)


def solution(mesh):
    in_specs = (
        P((WIDE, HUB), None),
        P((WIDE, HUB), None),
        P(),
        P(),
        P((WIDE, HUB), None, None),
        P((WIDE, HUB), None),
        P((WIDE, HUB)),
        P((WIDE, HUB)),
        P((WIDE, HUB)),
        P((WIDE, HUB)),
    )
    out_specs = (P((WIDE, HUB), None), P((WIDE, HUB), None), P(), P())
    return jax.shard_map(local, mesh=mesh, in_specs=in_specs, out_specs=out_specs, check_vma=False)
```

```python
import jax
import jax.numpy as jnp
from jax import lax
from jax.experimental import pallas as pl
from jax.experimental.pallas import tpu as pltpu
from jax.sharding import PartitionSpec as P

F32 = jnp.float32
BF16 = jnp.bfloat16
WIDE = "wide"
HUB = "hub"
LANES = 128
VMEM_BYTES = 16 * 1024 * 1024


def shaped(rows, cols, dtype):
    return jax.ShapeDtypeStruct((rows, cols), dtype)


def call(body, name, outs, ins, smem=(), traffic=1 << 20):
    spaces = [pltpu.SMEM if i in smem else pltpu.VMEM for i in range(len(ins))]
    return pl.pallas_call(
        body,
        name=name,
        out_shape=outs,
        in_specs=[pl.BlockSpec(memory_space=s) for s in spaces],
        out_specs=[pl.BlockSpec(memory_space=pltpu.VMEM) for _ in outs],
        cost_estimate=pl.CostEstimate(flops=0, bytes_accessed=traffic, transcendentals=0),
        compiler_params=pltpu.CompilerParams(vmem_limit_bytes=VMEM_BYTES),
    )(*ins)


def dot(a, b):
    return lax.dot_general(a, b, (((1,), (0,)), ((), ())), preferred_element_type=F32)


def dot_nt(a, b):
    return lax.dot_general(a, b, (((1,), (1,)), ((), ())), preferred_element_type=F32)


def dot_tn(a, b):
    return lax.dot_general(a, b, (((0,), (0,)), ((), ())), preferred_element_type=F32)


def to_wide(x, k):
    return lax.ppermute(x, WIDE, [(i, i ^ k) for i in range(lax.axis_size(WIDE))])


def to_both(x, k, j):
    n, m = lax.axis_size(WIDE), lax.axis_size(HUB)
    pairs = [(i * m + h, (i ^ k) * m + (h ^ j)) for i in range(n) for h in range(m)]
    return lax.ppermute(x, (WIDE, HUB), pairs)


def together(*values):
    return lax.optimization_barrier(values)


def gather_wide(own, beside=lambda: (), after=lambda early: ()):
    nz = lax.axis_size(WIDE) // 4
    zs = [to_wide(own, 4 * k) for k in range(1, nz)]
    xo = to_wide(own, 2)
    xo, early = together(xo, beside())
    xz = [to_wide(z, 2) for z in zs]
    near = [own, xo] + [p for pair in zip(zs, xz) for p in pair]
    late = after(early)
    return near + [to_wide(p, 1) for p in near], early, late


def pairwise(parts):
    while len(parts) > 1:
        parts = [parts[i] + parts[i + 1] for i in range(0, len(parts), 2)]
    return parts[0]


def tile_sum(adj_ref, piece_refs, rows=None):
    total = None
    for k, ref in enumerate(piece_refs):
        n = rows or ref.shape[0]
        term = dot(adj_ref[:, k * n : (k + 1) * n], ref[:n])
        total = term if total is None else total + term
    return total


def local(
    low_feats,
    hub_feats,
    w_first,
    w_second,
    low_tiles,
    tile_cols,
    edge_rows,
    edge_hubs,
    low_labels,
    hub_labels,
):
    rows, feat = low_feats.shape
    hr = hub_feats.shape[0]
    n_tiles, tile, _ = low_tiles.shape
    blocks = rows // tile
    per_block = n_tiles // blocks
    units = w_first.shape[1]
    classes = w_second.shape[1]
    n_wide, n_hub = lax.axis_size(WIDE), lax.axis_size(HUB)
    nz = n_wide // 4
    group = hr * n_hub
    total = (rows + hr) * n_wide * n_hub
    edges = edge_rows.shape[0]
    pay = feat + LANES

    at = [0]
    for n in (edges, edges, rows):
        at.append(at[-1] + n)
    ints = jnp.concatenate([edge_rows, edge_hubs, low_labels, hub_labels]).reshape(1, at[-1] + hr)

    def edge_tables(ints, feats, hub_rows, link, link_t, low_count, low_hot, hub_hot_out, *parts):
        e_rows, e_hubs, labels = (ints[:, at[i] : at[i + 1]] for i in range(3))
        labels_hub = ints[:, at[3] :]
        h = lax.axis_index(HUB)
        hubs = ((e_hubs // hr) ^ h) * hr + e_hubs % hr
        row_hot = (lax.broadcasted_iota(jnp.int32, (rows, edges), 0) == e_rows).astype(BF16)
        hub_hot = (lax.broadcasted_iota(jnp.int32, (group, edges), 0) == hubs).astype(BF16)
        links = dot_nt(hub_hot, row_hot)
        links_t = dot_nt(row_hot, hub_hot)
        hi, hi_t = links.astype(BF16), links_t.astype(BF16)
        lo, lo_t = (links - hi.astype(F32)).astype(BF16), (links_t - hi_t.astype(F32)).astype(BF16)
        link[:, :rows] = hi
        link[:, rows:] = lo
        link_t[...] = jnp.concatenate([hi_t, lo_t], axis=1)
        low_count[...] = jnp.broadcast_to(jnp.sum(links_t, axis=1, keepdims=True), (rows, LANES))
        sums = dot(hi, feats[...]) + dot(lo, feats[...])
        counts = jnp.broadcast_to(jnp.sum(links, axis=1, keepdims=True), (group, LANES))
        for k, part in enumerate(parts):
            part[:hr, :feat] = sums[k * hr : (k + 1) * hr]
            part[:hr, feat:] = counts[k * hr : (k + 1) * hr]
            part[hr:, :feat] = hub_rows[...].astype(F32)
            part[hr:, feat:] = jnp.zeros((hr, LANES), F32)
        hot = (lax.broadcasted_iota(jnp.int32, (classes, rows), 0) == labels).astype(F32)
        low_hot[...] = hot.T.astype(BF16)
        hot = (lax.broadcasted_iota(jnp.int32, (classes, hr), 0) == labels_hub).astype(F32)
        hub_hot_out[...] = hot.T.astype(BF16)

    link, link_t, low_count, low_target, hub_target, *parts1 = call(
        edge_tables,
        "edge_tables",
        [
            shaped(group, 2 * rows, BF16),
            shaped(rows, 2 * group, BF16),
            shaped(rows, LANES, F32),
            shaped(rows, classes, BF16),
            shaped(hr, classes, BF16),
        ]
        + [shaped(2 * hr, pay, F32) for _ in range(n_hub)],
        [ints, low_feats, hub_feats],
        traffic=4 << 20,
    )

    def adjacency(tiles, cols, low_count, adj, adj_t, scale):
        w = lax.axis_index(WIDE)
        adj[...] = jnp.zeros_like(adj)
        adj_t[...] = jnp.zeros_like(adj_t)
        for r in range(blocks):
            for k in range(per_block):
                b = cols[r, k]
                rel = (b // blocks) ^ w
                place = (rel & 1) * (n_wide // 2) + (rel >> 2) * 2 + ((rel >> 1) & 1)
                at = pl.ds(pl.multiple_of((place * blocks + b % blocks) * tile, tile), tile)
                value = tiles[r * per_block + k]
                adj[r * tile : (r + 1) * tile, at] = value
                adj_t[at, r * tile : (r + 1) * tile] = value.T
        deg = dot(adj[...], jnp.ones((n_wide * rows, LANES), BF16))
        scale[...] = lax.rsqrt(1.0 + deg + low_count[...])

    adj, adj_t, scale = call(
        adjacency,
        "adjacency",
        [shaped(rows, n_wide * rows, BF16), shaped(n_wide * rows, rows, BF16), shaped(rows, LANES, F32)],
        [low_tiles, tile_cols, low_count],
        smem=(1,),
        traffic=14 << 20,
    )

    def to_hub(x, k):
        return lax.ppermute(x, HUB, [(i, i ^ k) for i in range(n_hub)])

    mates = range(1, n_hub)

    def hub_first(feats, w, own, *refs):
        got, (hub_scale, agg, act) = refs[:-3], refs[-3:]
        sums = own[:hr]
        for g in got:
            sums = sums + g[:hr]
        s = lax.rsqrt(1.0 + sums[:, feat : feat + 1])
        hub_scale[...] = jnp.broadcast_to(s, (hr, LANES))
        a = ((feats[...].astype(F32) + sums[:, :feat]) * s).astype(BF16)
        agg[...] = a
        act[...] = jnp.maximum(dot(a, w[...]), 0.0).astype(BF16)

    def hubs_to_first(early):
        parts1 = early[0]
        got1 = [to_hub(parts1[k], k) for k in mates]
        outs = [shaped(hr, LANES, F32), shaped(hr, feat, BF16), shaped(hr, units, BF16)]
        return call(hub_first, "hub_first", outs, [hub_feats, w_first, parts1[0]] + got1), got1

    pieces1, (parts1, scale), ((hub_scale, agg1_hub, h1_hub), got1) = gather_wide(
        low_feats, lambda: (parts1, scale), hubs_to_first
    )
    n_pieces = len(pieces1)

    def low_first(adj, link, link_t, scale, field, w, act_hub, agg_hub, *refs):
        pieces, refs = refs[:n_pieces], refs[n_pieces:]
        hubs, (packed, own, *sends) = refs[:n_hub], refs[n_hub:]
        around = jnp.concatenate([r[hr:, :feat] for r in hubs] * 2, axis=0).astype(BF16)
        s = tile_sum(adj, pieces) + field[...].astype(F32) + dot(link_t[...], around)
        a = (s * scale[:, :1]).astype(BF16)
        act = jnp.maximum(dot(a, w[...]), 0.0).astype(BF16)
        packed[:rows] = act
        packed[rows:] = a.T
        sums = dot(link[:, :rows], act) + dot(link[:, rows:], act)
        own[...] = sums[:hr]
        for k, send in enumerate(sends, 1):
            send[:hr] = act_hub[...].astype(F32)
            send[hr : 2 * hr] = sums[k * hr : (k + 1) * hr]
            send[2 * hr :] = agg_hub[...].astype(F32)

    packed, own2, *sends2 = call(
        low_first,
        "low_first",
        [shaped(2 * rows, units, BF16), shaped(hr, units, F32)] + [shaped(3 * hr, units, F32) for _ in mates],
        [adj, link, link_t, scale, low_feats, w_first, h1_hub, agg1_hub] + pieces1 + [parts1[0]] + got1,
    )

    def hub_second(act, hub_scale, w, target, own, *refs):
        got, (logits, agg, dz, q) = refs[:-4], refs[-4:]
        sums = own[...]
        for g in got:
            sums = sums + g[hr : 2 * hr]
        s = hub_scale[:, :1]
        a = ((act[...].astype(F32) + sums) * s).astype(BF16)
        agg[...] = a
        y = dot(a, w[...])
        logits[...] = y
        d = ((y - target[...].astype(F32)) / total).astype(BF16)
        dz[...] = d
        q[...] = (dot_nt(d, w[...]) * s).astype(BF16)

    def hubs_to_second(got2):
        outs = [shaped(hr, classes, F32), shaped(hr, units, BF16), shaped(hr, classes, BF16), shaped(hr, units, BF16)]
        made = call(hub_second, "hub_second", outs, [h1_hub, hub_scale, w_second, hub_target, own2] + got2)
        return made, [to_hub(made[3], k) for k in mates]

    pieces2, got2, ((hub_logits, agg2_hub, dz2_hub, q_hub), q_hub_mates) = gather_wide(
        packed, lambda: [to_hub(x, k) for k, x in enumerate(sends2, 1)], hubs_to_second
    )

    def low_second(adj, link_t, scale, packed, w, target, act_hub, agg_hub, dz_hub, *refs):
        pieces, refs = refs[:n_pieces], refs[n_pieces:]
        got, (logits, grad, q_out) = refs[: n_hub - 1], refs[n_hub - 1 :]
        around = jnp.concatenate([act_hub[...]] + [g[:hr].astype(BF16) for g in got], axis=0)
        around = jnp.concatenate([around, around], axis=0)
        s = tile_sum(adj, pieces, rows) + packed[:rows].astype(F32) + dot(link_t[...], around)
        a = (s * scale[:, :1]).astype(BF16)
        y = dot(a, w[...])
        logits[...] = y
        d = ((y - target[...].astype(F32)) / total).astype(BF16)
        q_out[...] = (dot_nt(d, w[...]) * scale[:, :1]).astype(BF16)
        grad[...] = dot_tn(a, d) + dot_tn(agg_hub[...], dz_hub[...])

    low_logits, grad_second, q_low = call(
        low_second,
        "low_second",
        [shaped(rows, classes, F32), shaped(units, classes, F32), shaped(rows, units, BF16)],
        [adj, link_t, scale, packed, w_second, low_target, h1_hub, agg2_hub, dz2_hub] + pieces2 + got2,
    )

    def back_first(adj_t, link, link_t, q, grad_second, act_hub, agg_hub, q_hub, *refs):
        pieces, refs = refs[:n_pieces], refs[n_pieces:]
        got, refs = refs[: n_hub - 1], refs[n_hub - 1 :]
        q_mates, (keep, give) = refs[: n_hub - 1], refs[n_hub - 1 :]
        q_own = q[...]
        around = jnp.concatenate([q_hub[...]] + [g[...] for g in q_mates], axis=0)
        around = jnp.concatenate([around, around], axis=0)
        grad = None
        for k, piece in enumerate(pieces):
            term = dot(adj_t[k * rows : (k + 1) * rows], q_own)
            if k == 0:
                term = term + q_own.astype(F32) + dot(link_t[...], around)
            term = jnp.where(piece[:rows].astype(F32) > 0.0, term, 0.0).astype(BF16)
            term = dot(piece[rows:], term)
            grad = term if grad is None else grad + term
        sums = dot(link[:, :rows], q_own) + dot(link[:, rows:], q_own)
        for k in range(n_hub):
            term = sums[k * hr : (k + 1) * hr]
            act = act_hub[...].astype(F32) if k == 0 else got[k - 1][:hr]
            agg = agg_hub[...] if k == 0 else got[k - 1][2 * hr :].astype(BF16)
            if k == 0:
                term = term + q_hub[...].astype(F32)
            grad = grad + dot_tn(agg, jnp.where(act > 0.0, term, 0.0).astype(BF16))
        core = lax.axis_index(WIDE) & 1

        @pl.when(core == 0)
        def _():
            keep[...] = grad
            give[...] = grad_second[...]

        @pl.when(core == 1)
        def _():
            keep[...] = grad_second[...]
            give[...] = grad

    keep, give = call(
        back_first,
        "back_first",
        [shaped(units, classes, F32), shaped(units, classes, F32)],
        [adj_t, link, link_t, q_low, grad_second, h1_hub, agg1_hub, q_hub] + pieces2 + got2 + q_hub_mates,
    )
    got = to_wide(give, 1)

    n_share = 2 * n_hub
    share = units // n_share
    steps = [(2 * (k // n_hub), k % n_hub) for k in range(n_share)]

    def place_of():
        return ((lax.axis_index(WIDE) >> 1) & 1) * n_hub + lax.axis_index(HUB)

    def split(keep, got, *outs):
        me = place_of()
        for k, out in enumerate(outs):
            at = pl.ds(pl.multiple_of((me ^ k) * share, share), share)
            out[...] = keep[at] + got[at]

    shares = call(split, "split", [shaped(share, classes, F32) for _ in range(n_share)], [keep, got])
    shares = [shares[0]] + [to_both(shares[k], *steps[k]) for k in range(1, n_share)]

    def add_up(*refs):
        refs[-1][...] = pairwise([r[...] for r in refs[:-1]])

    (mine,) = call(add_up, "add_xy", [shaped(share, classes, F32)], shares)
    (mine,) = call(
        add_up, "add_z", [shaped(share, classes, F32)], [mine] + [to_wide(mine, 4 * k) for k in range(1, nz)]
    )
    mine = [mine] + [to_both(mine, *steps[k]) for k in range(1, n_share)]
    other = [to_wide(m, 1) for m in mine]

    def assemble(*refs):
        mine, other, (grad_first, grad_second) = refs[:n_share], refs[n_share : 2 * n_share], refs[2 * n_share :]
        me = place_of()
        core = lax.axis_index(WIDE) & 1

        def write(mine_out, other_out):
            for k in range(n_share):
                at = pl.ds(pl.multiple_of((me ^ k) * share, share), share)
                mine_out[at] = mine[k][...]
                other_out[at] = other[k][...]

        @pl.when(core == 0)
        def _():
            write(grad_first, grad_second)

        @pl.when(core == 1)
        def _():
            write(grad_second, grad_first)

    grad_first, grad_second = call(
        assemble, "assemble", [shaped(units, classes, F32), shaped(units, classes, F32)], mine + other
    )
    return (low_logits, hub_logits, grad_first, grad_second)


def solution(mesh):
    in_specs = (
        P((WIDE, HUB), None),
        P((WIDE, HUB), None),
        P(),
        P(),
        P((WIDE, HUB), None, None),
        P((WIDE, HUB), None),
        P((WIDE, HUB)),
        P((WIDE, HUB)),
        P((WIDE, HUB)),
        P((WIDE, HUB)),
    )
    out_specs = (P((WIDE, HUB), None), P((WIDE, HUB), None), P(), P())
    return jax.shard_map(local, mesh=mesh, in_specs=in_specs, out_specs=out_specs, check_vma=False)
```

```python
import jax
import jax.numpy as jnp
from jax import lax
from jax.experimental import pallas as pl
from jax.experimental.pallas import tpu as pltpu
from jax.sharding import PartitionSpec as P

F32 = jnp.float32
BF16 = jnp.bfloat16
WIDE = "wide"
HUB = "hub"
LANES = 128
VMEM_BYTES = 16 * 1024 * 1024


def shaped(rows, cols, dtype):
    return jax.ShapeDtypeStruct((rows, cols), dtype)


def call(body, name, outs, ins, smem=(), traffic=1 << 20):
    spaces = [pltpu.SMEM if i in smem else pltpu.VMEM for i in range(len(ins))]
    return pl.pallas_call(
        body,
        name=name,
        out_shape=outs,
        in_specs=[pl.BlockSpec(memory_space=s) for s in spaces],
        out_specs=[pl.BlockSpec(memory_space=pltpu.VMEM) for _ in outs],
        cost_estimate=pl.CostEstimate(flops=0, bytes_accessed=traffic, transcendentals=0),
        compiler_params=pltpu.CompilerParams(vmem_limit_bytes=VMEM_BYTES),
    )(*ins)


def dot(a, b):
    return lax.dot_general(a, b, (((1,), (0,)), ((), ())), preferred_element_type=F32)


def dot_nt(a, b):
    return lax.dot_general(a, b, (((1,), (1,)), ((), ())), preferred_element_type=F32)


def dot_tn(a, b):
    return lax.dot_general(a, b, (((0,), (0,)), ((), ())), preferred_element_type=F32)


def to_wide(x, k):
    return lax.ppermute(x, WIDE, [(i, i ^ k) for i in range(lax.axis_size(WIDE))])


def to_both(x, k, j):
    n, m = lax.axis_size(WIDE), lax.axis_size(HUB)
    pairs = [(i * m + h, (i ^ k) * m + (h ^ j)) for i in range(n) for h in range(m)]
    return lax.ppermute(x, (WIDE, HUB), pairs)


def together(*values):
    return lax.optimization_barrier(values)


def join(*parts):
    def body(*refs):
        at = 0
        for ref in refs[:-1]:
            refs[-1][at : at + ref.shape[0]] = ref[...]
            at += ref.shape[0]

    (out,) = call(body, "join", [shaped(sum(p.shape[0] for p in parts), parts[0].shape[1], parts[0].dtype)], parts)
    return out


def direct(nz):
    return [3, 1] + list(range(4, nz))


def over_z(own):
    return [to_wide(own, 4 * k) for k in direct(lax.axis_size(WIDE) // 4)]


def onward(over_x, over_z):
    return [to_wide(over_z[0], 4), to_wide(over_x, 8), to_wide(join(*over_z), 2)]


def place_of_block(z, x, nz):
    place = jnp.where(z == 2, nz + x, x)
    for at, k in enumerate(direct(nz), 2):
        place = jnp.where(z == k, at + x * nz, place)
    return place


def pairwise(parts):
    while len(parts) > 1:
        parts = [parts[i] + parts[i + 1] for i in range(0, len(parts), 2)]
    return parts[0]


def tile_sum(adj_ref, piece_refs):
    at, total = 0, None
    for ref in piece_refs:
        n = ref.shape[0]
        term = dot(adj_ref[:, at : at + n], ref[...])
        total = term if total is None else total + term
        at += n
    return total


def local(
    low_feats,
    hub_feats,
    w_first,
    w_second,
    low_tiles,
    tile_cols,
    edge_rows,
    edge_hubs,
    low_labels,
    hub_labels,
):
    rows, feat = low_feats.shape
    hr = hub_feats.shape[0]
    n_tiles, tile, _ = low_tiles.shape
    blocks = rows // tile
    per_block = n_tiles // blocks
    units = w_first.shape[1]
    classes = w_second.shape[1]
    n_wide, n_hub = lax.axis_size(WIDE), lax.axis_size(HUB)
    nz = n_wide // 4
    group = hr * n_hub
    total = (rows + hr) * n_wide * n_hub
    edges = edge_rows.shape[0]
    pay = feat + LANES
    half = n_wide * rows // 2

    feats_z, feats_x = over_z(low_feats), to_wide(low_feats, 2)

    mates = range(1, n_hub)

    def to_hub(x, k):
        return lax.ppermute(x, HUB, [(i, i ^ k) for i in range(n_hub)])

    at = [0]
    for n in (edges, edges, rows):
        at.append(at[-1] + n)
    ints = jnp.concatenate([edge_rows, edge_hubs, low_labels, hub_labels]).reshape(1, at[-1] + hr)

    def edge_tables(ints, feats, hub_rows, w, link, link_t, low_count, low_hot, hub_hot_out, feats_out, w_out, *parts):
        feats_out[...] = feats[...]
        w_out[...] = w[...]
        e_rows, e_hubs, labels = (ints[:, at[i] : at[i + 1]] for i in range(3))
        labels_hub = ints[:, at[3] :]
        h = lax.axis_index(HUB)
        hubs = ((e_hubs // hr) ^ h) * hr + e_hubs % hr
        row_hot = (lax.broadcasted_iota(jnp.int32, (rows, edges), 0) == e_rows).astype(BF16)
        hub_hot = (lax.broadcasted_iota(jnp.int32, (group, edges), 0) == hubs).astype(BF16)
        links = dot_nt(hub_hot, row_hot)
        links_t = dot_nt(row_hot, hub_hot)
        hi, hi_t = links.astype(BF16), links_t.astype(BF16)
        lo, lo_t = (links - hi.astype(F32)).astype(BF16), (links_t - hi_t.astype(F32)).astype(BF16)
        link[:, :rows] = hi
        link[:, rows:] = lo
        link_t[...] = jnp.concatenate([hi_t, lo_t], axis=1)
        low_count[...] = jnp.broadcast_to(jnp.sum(links_t, axis=1, keepdims=True), (rows, LANES))
        sums = dot(hi, feats[...]) + dot(lo, feats[...])
        counts = jnp.broadcast_to(jnp.sum(links, axis=1, keepdims=True), (group, LANES))
        for k, part in enumerate(parts):
            part[:hr, :feat] = sums[k * hr : (k + 1) * hr]
            part[:hr, feat:] = counts[k * hr : (k + 1) * hr]
            part[hr:, :feat] = hub_rows[...].astype(F32)
            part[hr:, feat:] = jnp.zeros((hr, LANES), F32)
        hot = (lax.broadcasted_iota(jnp.int32, (classes, rows), 0) == labels).astype(F32)
        low_hot[...] = hot.T.astype(BF16)
        hot = (lax.broadcasted_iota(jnp.int32, (classes, hr), 0) == labels_hub).astype(F32)
        hub_hot_out[...] = hot.T.astype(BF16)

    link, link_t, low_count, low_target, hub_target, near_feats, near_w, *parts1 = call(
        edge_tables,
        "edge_tables",
        [
            shaped(group, 2 * rows, BF16),
            shaped(rows, 2 * group, BF16),
            shaped(rows, LANES, F32),
            shaped(rows, classes, BF16),
            shaped(hr, classes, BF16),
            shaped(rows, feat, BF16),
            shaped(feat, units, BF16),
        ]
        + [shaped(2 * hr, pay, F32) for _ in range(n_hub)],
        [ints, low_feats, hub_feats, w_first],
        traffic=4 << 20,
    )

    feats_z, feats_x, parts1, low_count, near_feats, near_w = together(
        feats_z, feats_x, parts1, low_count, near_feats, near_w
    )
    feats_on = onward(feats_x, feats_z)
    feats_mate = [to_wide(join(near_feats, feats_x, *feats_z), 1)]

    def adjacency(tiles, cols, low_count, adj, adj_t, adj_t_give, scale):
        w = lax.axis_index(WIDE)
        adj[...] = jnp.zeros_like(adj)
        adj_t[...] = jnp.zeros_like(adj_t)
        adj_t_give[...] = jnp.zeros_like(adj_t_give)
        for r in range(blocks):
            for k in range(per_block):
                b = cols[r, k]
                rel = (b // blocks) ^ w
                place = place_of_block(rel >> 2, (rel >> 1) & 1, nz)
                start = pl.multiple_of((place * blocks + b % blocks) * tile, tile)
                value = tiles[r * per_block + k]
                turned = value.T
                at = pl.ds(pl.multiple_of((rel & 1) * half + start, tile), tile)
                adj[r * tile : (r + 1) * tile, at] = value

                @pl.when(rel & 1 == 0)
                def _():
                    adj_t[pl.ds(start, tile), r * tile : (r + 1) * tile] = turned

                @pl.when(rel & 1 == 1)
                def _():
                    adj_t_give[pl.ds(start, tile), r * tile : (r + 1) * tile] = turned

        deg = dot(adj[...], jnp.ones((2 * half, LANES), BF16))
        scale[...] = lax.rsqrt(1.0 + deg + low_count[...])

    adj, adj_t, adj_t_give, scale = call(
        adjacency,
        "adjacency",
        [shaped(rows, 2 * half, BF16), shaped(half, rows, BF16), shaped(half, rows, BF16), shaped(rows, LANES, F32)],
        [low_tiles, tile_cols, low_count],
        smem=(1,),
        traffic=14 << 20,
    )


    def hub_first(w, own, *refs):
        got, (hub_scale, agg, act) = refs[:-3], refs[-3:]
        sums = own[:hr]
        for g in got:
            sums = sums + g[:hr]
        s = lax.rsqrt(1.0 + sums[:, feat : feat + 1])
        hub_scale[...] = jnp.broadcast_to(s, (hr, LANES))
        a = ((own[hr:, :feat] + sums[:, :feat]) * s).astype(BF16)
        agg[...] = a
        act[...] = jnp.maximum(dot(a, w[...]), 0.0).astype(BF16)

    feats_on, feats_mate, scale, got1 = together(
        feats_on, feats_mate, scale, [to_hub(parts1[k], k) for k in mates]
    )
    feats_mate.append(to_wide(join(*feats_on), 1))
    pieces1 = [near_feats, feats_x] + feats_z + feats_on + feats_mate
    n_pieces = len(pieces1)
    hub_scale, agg1_hub, h1_hub = call(
        hub_first,
        "hub_first",
        [shaped(hr, LANES, F32), shaped(hr, feat, BF16), shaped(hr, units, BF16)],
        [near_w, parts1[0]] + got1,
    )
    def low_first(adj, link, link_t, scale, w, act_hub, agg_hub, *refs):
        pieces, refs = refs[:n_pieces], refs[n_pieces:]
        hubs, (act_out, turned, own, *sends) = refs[:n_hub], refs[n_hub:]
        around = jnp.concatenate([r[hr:, :feat] for r in hubs] * 2, axis=0).astype(BF16)
        s = tile_sum(adj, pieces) + pieces[0][...].astype(F32) + dot(link_t[...], around)
        a = (s * scale[:, :1]).astype(BF16)
        act = jnp.maximum(dot(a, w[...]), 0.0).astype(BF16)
        act_out[...] = act
        turned[...] = a.T
        sums = dot(link[:, :rows], act) + dot(link[:, rows:], act)
        own[...] = sums[:hr]
        for k, send in enumerate(sends, 1):
            send[:hr] = act_hub[...].astype(F32)
            send[hr : 2 * hr] = sums[k * hr : (k + 1) * hr]
            send[2 * hr :] = agg_hub[...].astype(F32)

    h1, agg1_t, own2, *sends2 = call(
        low_first,
        "low_first",
        [shaped(rows, units, BF16), shaped(feat, rows, BF16), shaped(hr, units, F32)]
        + [shaped(3 * hr, units, F32) for _ in mates],
        [adj, link, link_t, scale, near_w, h1_hub, agg1_hub] + pieces1 + [parts1[0]] + got1,
    )

    def hub_second(act, hub_scale, w, target, own, *refs):
        got, (logits, agg, dz, q) = refs[:-4], refs[-4:]
        sums = own[...]
        for g in got:
            sums = sums + g[hr : 2 * hr]
        s = hub_scale[:, :1]
        a = ((act[...].astype(F32) + sums) * s).astype(BF16)
        agg[...] = a
        y = dot(a, w[...])
        logits[...] = y
        d = ((y - target[...].astype(F32)) / total).astype(BF16)
        dz[...] = d
        q[...] = (dot_nt(d, w[...]) * s).astype(BF16)

    h1_z, h1_x, agg1_x, got2 = together(
        over_z(h1), to_wide(h1, 2), to_wide(agg1_t, 2), [to_hub(x, k) for k, x in enumerate(sends2, 1)]
    )
    hub_logits, agg2_hub, dz2_hub, q_hub = call(
        hub_second,
        "hub_second",
        [shaped(hr, classes, F32), shaped(hr, units, BF16), shaped(hr, classes, BF16), shaped(hr, units, BF16)],
        [h1_hub, hub_scale, w_second, hub_target, own2] + got2,
    )
    h1_on, agg1_z, q_hub, adj_t_give = together(onward(h1_x, h1_z), over_z(agg1_t), q_hub, adj_t_give)
    adj_t_mate = to_wide(adj_t_give, 1)
    agg1_on = onward(agg1_x, agg1_z)
    h1_mate = [to_wide(join(h1, h1_x, *h1_z, *h1_on), 1)]
    q_hub_mates = [to_hub(q_hub, k) for k in mates]
    pieces2 = [h1, h1_x] + h1_z + h1_on
    turned = [agg1_t, agg1_x] + agg1_z + agg1_on
    n_own = len(pieces2)

    def low_second(adj, link_t, scale, w, target, act_hub, agg_hub, dz_hub, *refs):
        pieces, refs = refs[: n_own + 1], refs[n_own + 1 :]
        got, (logits, grad, q_out) = refs[: n_hub - 1], refs[n_hub - 1 :]
        around = jnp.concatenate([act_hub[...]] + [g[:hr].astype(BF16) for g in got], axis=0)
        around = jnp.concatenate([around, around], axis=0)
        s = tile_sum(adj, pieces) + pieces[0][...].astype(F32) + dot(link_t[...], around)
        a = (s * scale[:, :1]).astype(BF16)
        y = dot(a, w[...])
        logits[...] = y
        d = ((y - target[...].astype(F32)) / total).astype(BF16)
        q_out[...] = (dot_nt(d, w[...]) * scale[:, :1]).astype(BF16)
        grad[...] = dot_tn(a, d) + dot_tn(agg_hub[...], dz_hub[...])

    low_logits, grad_second, q_low = call(
        low_second,
        "low_second",
        [shaped(rows, classes, F32), shaped(units, classes, F32), shaped(rows, units, BF16)],
        [adj, link_t, scale, w_second, low_target, h1_hub, agg2_hub, dz2_hub] + pieces2 + h1_mate + got2,
    )

    q_low, q_hub_mates = together(q_low, q_hub_mates)
    q_mate = to_wide(q_low, 1)

    def back_first(adj_t, adj_t_mate, link, link_t, q, q_mate, grad_second, act_hub, agg_hub, q_hub, *refs):
        pieces, refs = refs[:n_own], refs[n_own:]
        turned, refs = refs[:n_own], refs[n_own:]
        got, refs = refs[: n_hub - 1], refs[n_hub - 1 :]
        q_mates, (keep, give) = refs[: n_hub - 1], refs[n_hub - 1 :]
        q_own = q[...]
        around = jnp.concatenate([q_hub[...]] + [g[...] for g in q_mates], axis=0)
        around = jnp.concatenate([around, around], axis=0)
        grad, at = None, 0
        for piece, agg in zip(pieces, turned):
            for n in range(0, piece.shape[0], rows):
                term = dot(adj_t[at : at + rows], q_own) + dot(adj_t_mate[at : at + rows], q_mate[...])
                if at == 0:
                    term = term + q_own.astype(F32) + dot(link_t[...], around)
                term = jnp.where(piece[n : n + rows].astype(F32) > 0.0, term, 0.0).astype(BF16)
                term = dot(agg[n : n + feat], term)
                grad = term if grad is None else grad + term
                at += rows
        sums = dot(link[:, :rows], q_own) + dot(link[:, rows:], q_own)
        for k in range(n_hub):
            term = sums[k * hr : (k + 1) * hr]
            act = act_hub[...].astype(F32) if k == 0 else got[k - 1][:hr]
            agg = agg_hub[...] if k == 0 else got[k - 1][2 * hr :].astype(BF16)
            if k == 0:
                term = term + q_hub[...].astype(F32)
            grad = grad + dot_tn(agg, jnp.where(act > 0.0, term, 0.0).astype(BF16))
        core = lax.axis_index(WIDE) & 1

        @pl.when(core == 0)
        def _():
            keep[...] = grad
            give[...] = grad_second[...]

        @pl.when(core == 1)
        def _():
            keep[...] = grad_second[...]
            give[...] = grad

    keep, give = call(
        back_first,
        "back_first",
        [shaped(units, classes, F32), shaped(units, classes, F32)],
        [adj_t, adj_t_mate, link, link_t, q_low, q_mate, grad_second, h1_hub, agg1_hub, q_hub] + pieces2 + turned + got2 + q_hub_mates,
    )
    got = to_wide(give, 1)

    n_share = 2 * n_hub
    share = units // n_share
    steps = [(2 * (k // n_hub), k % n_hub) for k in range(n_share)]

    def place_of():
        return ((lax.axis_index(WIDE) >> 1) & 1) * n_hub + lax.axis_index(HUB)

    def split(keep, got, *outs):
        me = place_of()
        for k, out in enumerate(outs):
            at = pl.ds(pl.multiple_of((me ^ k) * share, share), share)
            out[...] = keep[at] + got[at]

    shares = call(split, "split", [shaped(share, classes, F32) for _ in range(n_share)], [keep, got])
    shares = [shares[0]] + [to_both(shares[k], *steps[k]) for k in range(1, n_share)]

    def add_up(*refs):
        refs[-1][...] = pairwise([r[...] for r in refs[:-1]])

    (mine,) = call(add_up, "add_xy", [shaped(share, classes, F32)], shares)
    (mine,) = call(
        add_up, "add_z", [shaped(share, classes, F32)], [mine] + [to_wide(mine, 4 * k) for k in range(1, nz)]
    )
    mine = [mine] + [to_both(mine, *steps[k]) for k in range(1, n_share)]
    other = [to_wide(m, 1) for m in mine]

    def assemble(*refs):
        mine, other, (grad_first, grad_second) = refs[:n_share], refs[n_share : 2 * n_share], refs[2 * n_share :]
        me = place_of()
        core = lax.axis_index(WIDE) & 1

        def write(mine_out, other_out):
            for k in range(n_share):
                at = pl.ds(pl.multiple_of((me ^ k) * share, share), share)
                mine_out[at] = mine[k][...]
                other_out[at] = other[k][...]

        @pl.when(core == 0)
        def _():
            write(grad_first, grad_second)

        @pl.when(core == 1)
        def _():
            write(grad_second, grad_first)

    grad_first, grad_second = call(
        assemble, "assemble", [shaped(units, classes, F32), shaped(units, classes, F32)], mine + other
    )
    return (low_logits, hub_logits, grad_first, grad_second)


def solution(mesh):
    in_specs = (
        P((WIDE, HUB), None),
        P((WIDE, HUB), None),
        P(),
        P(),
        P((WIDE, HUB), None, None),
        P((WIDE, HUB), None),
        P((WIDE, HUB)),
        P((WIDE, HUB)),
        P((WIDE, HUB)),
        P((WIDE, HUB)),
    )
    out_specs = (P((WIDE, HUB), None), P((WIDE, HUB), None), P(), P())
    return jax.shard_map(local, mesh=mesh, in_specs=in_specs, out_specs=out_specs, check_vma=False)
```

```python
import jax
import jax.numpy as jnp
from jax import lax
from jax.experimental import pallas as pl
from jax.experimental.pallas import tpu as pltpu
from jax.sharding import PartitionSpec as P

F32 = jnp.float32
BF16 = jnp.bfloat16
WIDE = "wide"
HUB = "hub"
LANES = 128
VMEM_BYTES = 16 * 1024 * 1024


def shaped(rows, cols, dtype):
    return jax.ShapeDtypeStruct((rows, cols), dtype)


def call(body, name, outs, ins, smem=(), traffic=1 << 20):
    spaces = [pltpu.SMEM if i in smem else pltpu.VMEM for i in range(len(ins))]
    return pl.pallas_call(
        body,
        name=name,
        out_shape=outs,
        in_specs=[pl.BlockSpec(memory_space=s) for s in spaces],
        out_specs=[pl.BlockSpec(memory_space=pltpu.VMEM) for _ in outs],
        cost_estimate=pl.CostEstimate(flops=0, bytes_accessed=traffic, transcendentals=0),
        compiler_params=pltpu.CompilerParams(vmem_limit_bytes=VMEM_BYTES),
    )(*ins)


def dot(a, b):
    return lax.dot_general(a, b, (((1,), (0,)), ((), ())), preferred_element_type=F32)


def dot_nt(a, b):
    return lax.dot_general(a, b, (((1,), (1,)), ((), ())), preferred_element_type=F32)


def dot_tn(a, b):
    return lax.dot_general(a, b, (((0,), (0,)), ((), ())), preferred_element_type=F32)


def to_wide(x, k):
    return lax.ppermute(x, WIDE, [(i, i ^ k) for i in range(lax.axis_size(WIDE))])


def to_both(x, k, j):
    n, m = lax.axis_size(WIDE), lax.axis_size(HUB)
    pairs = [(i * m + h, (i ^ k) * m + (h ^ j)) for i in range(n) for h in range(m)]
    return lax.ppermute(x, (WIDE, HUB), pairs)


def together(*values):
    return lax.optimization_barrier(values)


def join(*parts):
    def body(*refs):
        at = 0
        for ref in refs[:-1]:
            refs[-1][at : at + ref.shape[0]] = ref[...]
            at += ref.shape[0]

    (out,) = call(body, "join", [shaped(sum(p.shape[0] for p in parts), parts[0].shape[1], parts[0].dtype)], parts)
    return out


def direct(nz):
    return [3, 1] + list(range(4, nz))


def over_z(own):
    return [to_wide(own, 4 * k) for k in direct(lax.axis_size(WIDE) // 4)]


def onward(over_x, over_z, late=None):
    return [to_wide(over_x, 8), to_wide(over_z[0] if late is None else late, 4), to_wide(join(*over_z), 2)]


def place_of_block(z, x, nz):
    place = jnp.where(z == 2, nz + 1 - x, x)
    for at, k in enumerate(direct(nz), 2):
        place = jnp.where(z == k, at + x * nz, place)
    return place


def pairwise(parts):
    while len(parts) > 1:
        parts = [parts[i] + parts[i + 1] for i in range(0, len(parts), 2)]
    return parts[0]


def tile_sum(adj_ref, piece_refs):
    at, total = 0, None
    for ref in piece_refs:
        n = ref.shape[0]
        term = dot(adj_ref[:, at : at + n], ref[...])
        total = term if total is None else total + term
        at += n
    return total


def local(
    low_feats,
    hub_feats,
    w_first,
    w_second,
    low_tiles,
    tile_cols,
    edge_rows,
    edge_hubs,
    low_labels,
    hub_labels,
):
    rows, feat = low_feats.shape
    hr = hub_feats.shape[0]
    n_tiles, tile, _ = low_tiles.shape
    blocks = rows // tile
    per_block = n_tiles // blocks
    units = w_first.shape[1]
    classes = w_second.shape[1]
    n_wide, n_hub = lax.axis_size(WIDE), lax.axis_size(HUB)
    nz = n_wide // 4
    group = hr * n_hub
    total = (rows + hr) * n_wide * n_hub
    edges = edge_rows.shape[0]
    pay = feat + LANES
    half = n_wide * rows // 2

    feats_z, feats_x = over_z(low_feats), to_wide(low_feats, 2)

    mates = range(1, n_hub)

    def to_hub(x, k):
        return lax.ppermute(x, HUB, [(i, i ^ k) for i in range(n_hub)])

    at = [0]
    for n in (edges, edges, rows):
        at.append(at[-1] + n)
    ints = jnp.concatenate([edge_rows, edge_hubs, low_labels, hub_labels]).reshape(1, at[-1] + hr)

    def edge_tables(ints, feats, hub_rows, w, link, link_t, low_count, low_hot, feats_out, w_out, part):
        feats_out[...] = feats[...]
        w_out[...] = w[...]
        e_rows, e_hubs, labels = (ints[:, at[i] : at[i + 1]] for i in range(3))
        labels_hub = ints[:, at[3] :]
        h = lax.axis_index(HUB)
        hubs = ((e_hubs // hr) ^ h) * hr + e_hubs % hr
        row_hot = (lax.broadcasted_iota(jnp.int32, (rows, edges), 0) == e_rows).astype(BF16)
        hub_hot = (lax.broadcasted_iota(jnp.int32, (group, edges), 0) == hubs).astype(BF16)
        links = dot_nt(hub_hot, row_hot)
        links_t = dot_nt(row_hot, hub_hot)
        hi, hi_t = links.astype(BF16), links_t.astype(BF16)
        lo, lo_t = (links - hi.astype(F32)).astype(BF16), (links_t - hi_t.astype(F32)).astype(BF16)
        link[:, :rows] = hi
        link[:, rows:] = lo
        link_t[...] = jnp.concatenate([hi_t, lo_t], axis=1)
        low_count[...] = jnp.broadcast_to(jnp.sum(links_t, axis=1, keepdims=True), (rows, LANES))
        sums = dot(hi, feats[...]) + dot(lo, feats[...])
        counts = jnp.broadcast_to(jnp.sum(links, axis=1, keepdims=True), (group, LANES))
        part[:group, :feat] = sums
        part[:group, feat:] = counts
        part[group:, :feat] = hub_rows[...].astype(F32)
        part[group:, feat:] = jnp.broadcast_to(labels_hub.astype(F32), (LANES, hr)).T
        hot = (lax.broadcasted_iota(jnp.int32, (classes, rows), 0) == labels).astype(F32)
        low_hot[...] = hot.T.astype(BF16)

    link, link_t, low_count, low_target, near_feats, near_w, part1 = call(
        edge_tables,
        "edge_tables",
        [
            shaped(group, 2 * rows, BF16),
            shaped(rows, 2 * group, BF16),
            shaped(rows, LANES, F32),
            shaped(rows, classes, BF16),
            shaped(rows, feat, BF16),
            shaped(feat, units, BF16),
            shaped(group + hr, pay, F32),
        ],
        [ints, low_feats, hub_feats, w_first],
        traffic=4 << 20,
    )

    feats_z, feats_x, part1, low_count, near_feats, near_w = together(
        feats_z, feats_x, part1, low_count, near_feats, near_w
    )
    feats_on = onward(feats_x, feats_z)
    feats_mate = [to_wide(join(near_feats, feats_x, *feats_z), 1)]

    def adjacency(tiles, cols, low_count, adj, adj_t, adj_t_give, scale):
        w = lax.axis_index(WIDE)
        adj[...] = jnp.zeros_like(adj)
        adj_t[...] = jnp.zeros_like(adj_t)
        adj_t_give[...] = jnp.zeros_like(adj_t_give)
        for r in range(blocks):
            for k in range(per_block):
                b = cols[r, k]
                rel = (b // blocks) ^ w
                place = place_of_block(rel >> 2, (rel >> 1) & 1, nz)
                start = pl.multiple_of((place * blocks + b % blocks) * tile, tile)
                value = tiles[r * per_block + k]
                turned = value.T
                at = pl.ds(pl.multiple_of((rel & 1) * half + start, tile), tile)
                adj[r * tile : (r + 1) * tile, at] = value

                @pl.when(rel & 1 == 0)
                def _():
                    adj_t[pl.ds(start, tile), r * tile : (r + 1) * tile] = turned

                @pl.when(rel & 1 == 1)
                def _():
                    adj_t_give[pl.ds(start, tile), r * tile : (r + 1) * tile] = turned

        deg = dot(adj[...], jnp.ones((2 * half, LANES), BF16))
        scale[...] = lax.rsqrt(1.0 + deg + low_count[...])

    adj, adj_t, adj_t_give, scale = call(
        adjacency,
        "adjacency",
        [shaped(rows, 2 * half, BF16), shaped(half, rows, BF16), shaped(half, rows, BF16), shaped(rows, LANES, F32)],
        [low_tiles, tile_cols, low_count],
        smem=(1,),
        traffic=14 << 20,
    )


    def group_sum(own, got):
        blocks = []
        for m in range(n_hub):
            block = own[m * hr : (m + 1) * hr]
            for k, g in enumerate(got, 1):
                block = block + g[(m ^ k) * hr : ((m ^ k) + 1) * hr]
            blocks.append(block)
        return jnp.concatenate(blocks, axis=0)

    def hub_first(w, own, *refs):
        got, (hub_scale, field, agg, act, target) = refs[:-5], refs[-5:]
        sums = group_sum(own, got)
        rest = jnp.concatenate([r[group:] for r in (own, *got)], axis=0)
        s = lax.rsqrt(1.0 + sums[:, feat : feat + 1])
        hub_scale[...] = jnp.broadcast_to(s, (group, LANES))
        field[...] = rest[:, :feat].astype(BF16)
        a = ((rest[:, :feat] + sums[:, :feat]) * s).astype(BF16)
        agg[...] = a
        act[...] = jnp.maximum(dot(a, w[...]), 0.0).astype(BF16)
        labels = rest[:, feat : feat + 1].astype(jnp.int32)
        target[...] = (lax.broadcasted_iota(jnp.int32, (group, classes), 1) == labels).astype(BF16)

    feats_on, feats_mate, scale, got1 = together(
        feats_on, feats_mate, scale, [to_hub(part1, k) for k in mates]
    )
    feats_mate.append(to_wide(join(*feats_on), 1))
    pieces1 = [near_feats, feats_x] + feats_z + feats_on + feats_mate
    hub_scale, hub_field, agg1_hub, h1_hub, hub_target = call(
        hub_first,
        "hub_first",
        [
            shaped(group, LANES, F32),
            shaped(group, feat, BF16),
            shaped(group, feat, BF16),
            shaped(group, units, BF16),
            shaped(group, classes, BF16),
        ],
        [near_w, part1] + got1,
    )

    def low_near(adj, link_t, around, *refs):
        pieces, out = refs[:-1], refs[-1]
        around = jnp.concatenate([around[...], around[...]], axis=0)
        out[...] = tile_sum(adj, pieces) + pieces[0][...].astype(F32) + dot(link_t[...], around)

    (sum_near,) = call(
        low_near, "low_near", [shaped(rows, feat, F32)], [adj, link_t, hub_field] + pieces1[:-1]
    )

    def low_first(adj, link, scale, w, sum_near, last, act_out, turned, sums):
        s = sum_near[...] + dot(adj[:, 2 * half - last.shape[0] :], last[...])
        a = (s * scale[:, :1]).astype(BF16)
        act = jnp.maximum(dot(a, w[...]), 0.0).astype(BF16)
        act_out[...] = act
        turned[...] = a.T
        sums[...] = dot(link[:, :rows], act) + dot(link[:, rows:], act)

    h1, agg1_t, part2 = call(
        low_first,
        "low_first",
        [shaped(rows, units, BF16), shaped(feat, rows, BF16), shaped(group, units, F32)],
        [adj, link, scale, near_w, sum_near, pieces1[-1]],
    )

    def hub_second(act, hub_scale, w, target, own, *refs):
        got, (logits, agg, dz, q) = refs[:-4], refs[-4:]
        s = hub_scale[:, :1]
        a = ((act[...].astype(F32) + group_sum(own, got)) * s).astype(BF16)
        y = dot(a, w[...])
        d = ((y - target[...].astype(F32)) / total).astype(BF16)
        agg[...] = a[:hr]
        logits[...] = y[:hr]
        dz[...] = d[:hr]
        q[...] = (dot_nt(d, w[...]) * s).astype(BF16)

    h1_z, h1_x = together(over_z(h1), to_wide(h1, 2))
    got2 = [to_hub(part2, k) for k in mates]
    agg1_z, agg1_x, h1_z_late = together(over_z(agg1_t), to_wide(agg1_t, 2), h1_z[0])
    h1_on = onward(h1_x, h1_z, h1_z_late)
    h1_on, adj_t_give, got2 = together(h1_on, adj_t_give, got2)
    hub_logits, agg2_hub, dz2_hub, q_hub = call(
        hub_second,
        "hub_second",
        [shaped(hr, classes, F32), shaped(hr, units, BF16), shaped(hr, classes, BF16), shaped(group, units, BF16)],
        [h1_hub, hub_scale, w_second, hub_target, part2] + got2,
    )
    adj_t_mate = to_wide(adj_t_give, 1)
    agg1_on = onward(agg1_x, agg1_z)
    h1_mate = [to_wide(join(h1, h1_x, *h1_z, *h1_on), 1)]
    pieces2 = [h1, h1_x] + h1_z + h1_on
    turned = [agg1_t, agg1_x] + agg1_z + agg1_on
    n_own = len(pieces2)

    def low_second(adj, link_t, scale, w, target, act_hub, *refs):
        pieces, (logits, grad, q_out) = refs[: n_own + 1], refs[n_own + 1 :]
        around = jnp.concatenate([act_hub[...], act_hub[...]], axis=0)
        s = tile_sum(adj, pieces) + pieces[0][...].astype(F32) + dot(link_t[...], around)
        a = (s * scale[:, :1]).astype(BF16)
        y = dot(a, w[...])
        logits[...] = y
        d = ((y - target[...].astype(F32)) / total).astype(BF16)
        q_out[...] = (dot_nt(d, w[...]) * scale[:, :1]).astype(BF16)
        grad[...] = dot_tn(a, d)

    low_logits, grad_second, q_low = call(
        low_second,
        "low_second",
        [shaped(rows, classes, F32), shaped(units, classes, F32), shaped(rows, units, BF16)],
        [adj, link_t, scale, w_second, low_target, h1_hub] + pieces2 + h1_mate,
    )

    q_mate = to_wide(q_low, 1)

    def back_first(
        adj_t, adj_t_mate, link, link_t, q, q_mate, grad_low, act_hub, agg_hub, q_hub, agg2_hub, dz_hub, *refs
    ):
        pieces, refs = refs[:n_own], refs[n_own:]
        turned, (keep, give) = refs[:n_own], refs[n_own:]
        q_own = q[...]
        around = jnp.concatenate([q_hub[...], q_hub[...]], axis=0)
        grad, at = None, 0
        for piece, agg in zip(pieces, turned):
            for n in range(0, piece.shape[0], rows):
                term = dot(adj_t[at : at + rows], q_own) + dot(adj_t_mate[at : at + rows], q_mate[...])
                if at == 0:
                    term = term + q_own.astype(F32) + dot(link_t[...], around)
                term = jnp.where(piece[n : n + rows].astype(F32) > 0.0, term, 0.0).astype(BF16)
                term = dot(agg[n : n + feat], term)
                grad = term if grad is None else grad + term
                at += rows
        sums = dot(link[:, :rows], q_own) + dot(link[:, rows:], q_own)
        mine = lax.broadcasted_iota(jnp.int32, (group, units), 0) < hr
        sums = sums + jnp.where(mine, q_hub[...].astype(F32), 0.0)
        sums = jnp.where(act_hub[...].astype(F32) > 0.0, sums, 0.0).astype(BF16)
        grad = grad + dot_tn(agg_hub[...], sums)
        grad_second = grad_low[...] + dot_tn(agg2_hub[...], dz_hub[...])
        core = lax.axis_index(WIDE) & 1

        @pl.when(core == 0)
        def _():
            keep[...] = grad
            give[...] = grad_second

        @pl.when(core == 1)
        def _():
            keep[...] = grad_second
            give[...] = grad

    keep, give = call(
        back_first,
        "back_first",
        [shaped(units, classes, F32), shaped(units, classes, F32)],
        [adj_t, adj_t_mate, link, link_t, q_low, q_mate, grad_second, h1_hub, agg1_hub, q_hub, agg2_hub, dz2_hub]
        + pieces2
        + turned,
    )
    got = to_wide(give, 1)

    n_share = 2 * n_hub
    share = units // n_share
    steps = [(2 * (k // n_hub), k % n_hub) for k in range(n_share)]

    def place_of():
        return ((lax.axis_index(WIDE) >> 1) & 1) * n_hub + lax.axis_index(HUB)

    def split(keep, got, *outs):
        me = place_of()
        for k, out in enumerate(outs):
            at = pl.ds(pl.multiple_of((me ^ k) * share, share), share)
            out[...] = keep[at] + got[at]

    shares = call(split, "split", [shaped(share, classes, F32) for _ in range(n_share)], [keep, got])
    shares = [to_both(shares[k], *steps[k]) for k in range(n_share - 1, 0, -1)] + [shares[0]]

    def add_up(*refs):
        refs[-1][...] = pairwise([r[...] for r in refs[:-1]])

    (mine,) = call(add_up, "add_xy", [shaped(share, classes, F32)], shares)
    parts = [mine] + [to_wide(mine, 4 * k) for k in range(1, nz)]
    (mine,) = call(add_up, "add_z", [shaped(share, classes, F32)], parts)
    mine = [to_both(mine, *steps[k]) for k in range(n_share - 1, 0, -1)] + [mine]
    other = [to_wide(m, 1) for m in mine]

    def assemble(*refs):
        mine, other, (grad_first, grad_second) = refs[:n_share], refs[n_share : 2 * n_share], refs[2 * n_share :]
        me = place_of()
        core = lax.axis_index(WIDE) & 1

        def write(mine_out, other_out):
            for k in range(n_share):
                at = pl.ds(pl.multiple_of((me ^ (n_share - 1 - k)) * share, share), share)
                mine_out[at] = mine[k][...]
                other_out[at] = other[k][...]

        @pl.when(core == 0)
        def _():
            write(grad_first, grad_second)

        @pl.when(core == 1)
        def _():
            write(grad_second, grad_first)

    grad_first, grad_second = call(
        assemble, "assemble", [shaped(units, classes, F32), shaped(units, classes, F32)], mine + other
    )
    return (low_logits, hub_logits, grad_first, grad_second)


def solution(mesh):
    in_specs = (
        P((WIDE, HUB), None),
        P((WIDE, HUB), None),
        P(),
        P(),
        P((WIDE, HUB), None, None),
        P((WIDE, HUB), None),
        P((WIDE, HUB)),
        P((WIDE, HUB)),
        P((WIDE, HUB)),
        P((WIDE, HUB)),
    )
    out_specs = (P((WIDE, HUB), None), P((WIDE, HUB), None), P(), P())
    return jax.shard_map(local, mesh=mesh, in_specs=in_specs, out_specs=out_specs, check_vma=False)
```

```python
import jax
import jax.numpy as jnp
from jax import lax
from jax.experimental import pallas as pl
from jax.experimental.pallas import tpu as pltpu
from jax.sharding import PartitionSpec as P

F32 = jnp.float32
BF16 = jnp.bfloat16
WIDE = "wide"
HUB = "hub"
LANES = 128
VMEM_BYTES = 16 * 1024 * 1024


def shaped(rows, cols, dtype):
    return jax.ShapeDtypeStruct((rows, cols), dtype)


def call(body, name, outs, ins, smem=(), traffic=1 << 20):
    spaces = [pltpu.SMEM if i in smem else pltpu.VMEM for i in range(len(ins))]
    return pl.pallas_call(
        body,
        name=name,
        out_shape=outs,
        in_specs=[pl.BlockSpec(memory_space=s) for s in spaces],
        out_specs=[pl.BlockSpec(memory_space=pltpu.VMEM) for _ in outs],
        cost_estimate=pl.CostEstimate(flops=0, bytes_accessed=traffic, transcendentals=0),
        compiler_params=pltpu.CompilerParams(vmem_limit_bytes=VMEM_BYTES),
    )(*ins)


def dot(a, b):
    return lax.dot_general(a, b, (((1,), (0,)), ((), ())), preferred_element_type=F32)


def dot_nt(a, b):
    return lax.dot_general(a, b, (((1,), (1,)), ((), ())), preferred_element_type=F32)


def dot_tn(a, b):
    return lax.dot_general(a, b, (((0,), (0,)), ((), ())), preferred_element_type=F32)


def to_wide(x, k):
    return lax.ppermute(x, WIDE, [(i, i ^ k) for i in range(lax.axis_size(WIDE))])


def to_both(x, k, j):
    n, m = lax.axis_size(WIDE), lax.axis_size(HUB)
    pairs = [(i * m + h, (i ^ k) * m + (h ^ j)) for i in range(n) for h in range(m)]
    return lax.ppermute(x, (WIDE, HUB), pairs)


def together(*values):
    return lax.optimization_barrier(values)


def join(*parts):
    def body(*refs):
        at = 0
        for ref in refs[:-1]:
            refs[-1][at : at + ref.shape[0]] = ref[...]
            at += ref.shape[0]

    (out,) = call(body, "join", [shaped(sum(p.shape[0] for p in parts), parts[0].shape[1], parts[0].dtype)], parts)
    return out


def direct(nz):
    return [3, 1] + list(range(4, nz))


def over_z(own):
    return [to_wide(own, 4 * k) for k in direct(lax.axis_size(WIDE) // 4)]


def onward(over_x, over_z, late=None):
    return [to_wide(over_x, 8), to_wide(over_z[0] if late is None else late, 4), to_wide(join(*over_z), 2)]


def place_of_block(z, x, nz):
    place = jnp.where(z == 2, nz + 1 - x, x)
    for at, k in enumerate(direct(nz), 2):
        place = jnp.where(z == k, at + x * nz, place)
    return place


def pairwise(parts):
    while len(parts) > 1:
        parts = [parts[i] + parts[i + 1] for i in range(0, len(parts), 2)]
    return parts[0]


def tile_sum(adj_ref, piece_refs):
    at, total = 0, None
    for ref in piece_refs:
        n = ref.shape[0]
        term = dot(adj_ref[:, at : at + n], ref[...])
        total = term if total is None else total + term
        at += n
    return total


def local(
    low_feats,
    hub_feats,
    w_first,
    w_second,
    low_tiles,
    tile_cols,
    edge_rows,
    edge_hubs,
    low_labels,
    hub_labels,
):
    rows, feat = low_feats.shape
    hr = hub_feats.shape[0]
    n_tiles, tile, _ = low_tiles.shape
    blocks = rows // tile
    per_block = n_tiles // blocks
    units = w_first.shape[1]
    classes = w_second.shape[1]
    n_wide, n_hub = lax.axis_size(WIDE), lax.axis_size(HUB)
    nz = n_wide // 4
    group = hr * n_hub
    total = (rows + hr) * n_wide * n_hub
    edges = edge_rows.shape[0]
    pay = feat + LANES
    half = n_wide * rows // 2

    feats_z, feats_x = over_z(low_feats), to_wide(low_feats, 2)

    mates = range(1, n_hub)

    def to_hub(x, k):
        return lax.ppermute(x, HUB, [(i, i ^ k) for i in range(n_hub)])

    at = [0]
    for n in (edges, edges, rows):
        at.append(at[-1] + n)
    ints = jnp.concatenate([edge_rows, edge_hubs, low_labels, hub_labels]).reshape(1, at[-1] + hr)

    def edge_tables(ints, feats, hub_rows, w, link, link_t, low_count, low_hot, feats_out, w_out, part):
        feats_out[...] = feats[...]
        w_out[...] = w[...]
        e_rows, e_hubs, labels = (ints[:, at[i] : at[i + 1]] for i in range(3))
        labels_hub = ints[:, at[3] :]
        h = lax.axis_index(HUB)
        hubs = ((e_hubs // hr) ^ h) * hr + e_hubs % hr
        row_hot = (lax.broadcasted_iota(jnp.int32, (rows, edges), 0) == e_rows).astype(BF16)
        hub_hot = (lax.broadcasted_iota(jnp.int32, (group, edges), 0) == hubs).astype(BF16)
        links = dot_nt(hub_hot, row_hot)
        links_t = dot_nt(row_hot, hub_hot)
        hi, hi_t = links.astype(BF16), links_t.astype(BF16)
        lo, lo_t = (links - hi.astype(F32)).astype(BF16), (links_t - hi_t.astype(F32)).astype(BF16)
        link[:, :rows] = hi
        link[:, rows:] = lo
        link_t[...] = jnp.concatenate([hi_t, lo_t], axis=1)
        low_count[...] = jnp.broadcast_to(jnp.sum(links_t, axis=1, keepdims=True), (rows, LANES))
        sums = dot(hi, feats[...]) + dot(lo, feats[...])
        counts = jnp.broadcast_to(jnp.sum(links, axis=1, keepdims=True), (group, LANES))
        part[:group, :feat] = sums
        part[:group, feat:] = counts
        part[group:, :feat] = hub_rows[...].astype(F32)
        part[group:, feat:] = jnp.broadcast_to(labels_hub.astype(F32), (LANES, hr)).T
        hot = (lax.broadcasted_iota(jnp.int32, (classes, rows), 0) == labels).astype(F32)
        low_hot[...] = hot.T.astype(BF16)

    link, link_t, low_count, low_target, near_feats, near_w, part1 = call(
        edge_tables,
        "edge_tables",
        [
            shaped(group, 2 * rows, BF16),
            shaped(rows, 2 * group, BF16),
            shaped(rows, LANES, F32),
            shaped(rows, classes, BF16),
            shaped(rows, feat, BF16),
            shaped(feat, units, BF16),
            shaped(group + hr, pay, F32),
        ],
        [ints, low_feats, hub_feats, w_first],
        traffic=4 << 20,
    )

    feats_z, feats_x, part1, low_count, near_feats, near_w = together(
        feats_z, feats_x, part1, low_count, near_feats, near_w
    )
    feats_on = onward(feats_x, feats_z)
    feats_mate = [to_wide(join(near_feats, feats_x, *feats_z), 1)]

    def adjacency(tiles, cols, low_count, adj, adj_t, adj_t_give, scale):
        w = lax.axis_index(WIDE)
        adj[...] = jnp.zeros_like(adj)
        adj_t[...] = jnp.zeros_like(adj_t)
        adj_t_give[...] = jnp.zeros_like(adj_t_give)
        for r in range(blocks):
            for k in range(per_block):
                b = cols[r, k]
                rel = (b // blocks) ^ w
                place = place_of_block(rel >> 2, (rel >> 1) & 1, nz)
                start = pl.multiple_of((place * blocks + b % blocks) * tile, tile)
                value = tiles[r * per_block + k]
                turned = value.T
                at = pl.ds(pl.multiple_of((rel & 1) * half + start, tile), tile)
                adj[r * tile : (r + 1) * tile, at] = value

                @pl.when(rel & 1 == 0)
                def _():
                    adj_t[pl.ds(start, tile), r * tile : (r + 1) * tile] = turned

                @pl.when(rel & 1 == 1)
                def _():
                    adj_t_give[pl.ds(start, tile), r * tile : (r + 1) * tile] = turned

        deg = dot(adj[...], jnp.ones((2 * half, LANES), BF16))
        scale[...] = lax.rsqrt(1.0 + deg + low_count[...])

    adj, adj_t, adj_t_give, scale = call(
        adjacency,
        "adjacency",
        [shaped(rows, 2 * half, BF16), shaped(half, rows, BF16), shaped(half, rows, BF16), shaped(rows, LANES, F32)],
        [low_tiles, tile_cols, low_count],
        smem=(1,),
        traffic=14 << 20,
    )


    def group_sum(own, got):
        blocks = []
        for m in range(n_hub):
            block = own[m * hr : (m + 1) * hr]
            for k, g in enumerate(got, 1):
                block = block + g[(m ^ k) * hr : ((m ^ k) + 1) * hr]
            blocks.append(block)
        return jnp.concatenate(blocks, axis=0)

    def hub_first(w, own, *refs):
        got, (hub_scale, field, agg, act, target) = refs[:-5], refs[-5:]
        sums = group_sum(own, got)
        rest = jnp.concatenate([r[group:] for r in (own, *got)], axis=0)
        s = lax.rsqrt(1.0 + sums[:, feat : feat + 1])
        hub_scale[...] = jnp.broadcast_to(s, (group, LANES))
        field[...] = rest[:, :feat].astype(BF16)
        a = ((rest[:, :feat] + sums[:, :feat]) * s).astype(BF16)
        agg[...] = a
        act[...] = jnp.maximum(dot(a, w[...]), 0.0).astype(BF16)
        labels = rest[:, feat : feat + 1].astype(jnp.int32)
        target[...] = (lax.broadcasted_iota(jnp.int32, (group, classes), 1) == labels).astype(BF16)

    feats_on, scale, got1 = together(
        feats_on, scale, [to_hub(part1, k) for k in mates]
    )
    feats_mate.append(to_wide(join(*feats_on), 1))
    pieces1 = [near_feats, feats_x] + feats_z + feats_on + feats_mate
    hub_scale, hub_field, agg1_hub, h1_hub, hub_target = call(
        hub_first,
        "hub_first",
        [
            shaped(group, LANES, F32),
            shaped(group, feat, BF16),
            shaped(group, feat, BF16),
            shaped(group, units, BF16),
            shaped(group, classes, BF16),
        ],
        [near_w, part1] + got1,
    )

    def low_near(adj, link_t, around, *refs):
        pieces, out = refs[:-1], refs[-1]
        around = jnp.concatenate([around[...], around[...]], axis=0)
        out[...] = tile_sum(adj, pieces) + pieces[0][...].astype(F32) + dot(link_t[...], around)

    (sum_near,) = call(
        low_near, "low_near", [shaped(rows, feat, F32)], [adj, link_t, hub_field] + pieces1[:-1]
    )

    def low_first(adj, link, scale, w, sum_near, last, act_out, turned, sums):
        s = sum_near[...] + dot(adj[:, 2 * half - last.shape[0] :], last[...])
        a = (s * scale[:, :1]).astype(BF16)
        act = jnp.maximum(dot(a, w[...]), 0.0).astype(BF16)
        act_out[...] = act
        turned[...] = a.T
        sums[...] = dot(link[:, :rows], act) + dot(link[:, rows:], act)

    h1, agg1_t, part2 = call(
        low_first,
        "low_first",
        [shaped(rows, units, BF16), shaped(feat, rows, BF16), shaped(group, units, F32)],
        [adj, link, scale, near_w, sum_near, pieces1[-1]],
    )

    def hub_second(act, hub_scale, w, target, own, *refs):
        got, (logits, agg, dz, q) = refs[:-4], refs[-4:]
        s = hub_scale[:, :1]
        a = ((act[...].astype(F32) + group_sum(own, got)) * s).astype(BF16)
        y = dot(a, w[...])
        d = ((y - target[...].astype(F32)) / total).astype(BF16)
        agg[...] = a[:hr]
        logits[...] = y[:hr]
        dz[...] = d[:hr]
        q[...] = (dot_nt(d, w[...]) * s).astype(BF16)

    h1_z, h1_x = together(over_z(h1), to_wide(h1, 2))
    agg1_z, agg1_x, h1_z_late = together(over_z(agg1_t), to_wide(agg1_t, 2), h1_z[0])
    part2_late, _ = together(part2, agg1_x)
    got2 = [to_hub(part2_late, k) for k in mates]
    h1_on = onward(h1_x, h1_z, h1_z_late)
    h1_on, adj_t_give, got2 = together(h1_on, adj_t_give, got2)
    hub_logits, agg2_hub, dz2_hub, q_hub = call(
        hub_second,
        "hub_second",
        [shaped(hr, classes, F32), shaped(hr, units, BF16), shaped(hr, classes, BF16), shaped(group, units, BF16)],
        [h1_hub, hub_scale, w_second, hub_target, part2] + got2,
    )
    adj_t_mate = to_wide(adj_t_give, 1)
    agg1_on = onward(agg1_x, agg1_z)
    h1_mate = [to_wide(join(h1, h1_x, *h1_z, *h1_on), 1)]
    pieces2 = [h1, h1_x] + h1_z + h1_on
    turned = [agg1_t, agg1_x] + agg1_z + agg1_on
    n_own = len(pieces2)

    def low_second(adj, link_t, scale, w, target, act_hub, *refs):
        pieces, (logits, grad, q_out) = refs[: n_own + 1], refs[n_own + 1 :]
        around = jnp.concatenate([act_hub[...], act_hub[...]], axis=0)
        s = tile_sum(adj, pieces) + pieces[0][...].astype(F32) + dot(link_t[...], around)
        a = (s * scale[:, :1]).astype(BF16)
        y = dot(a, w[...])
        logits[...] = y
        d = ((y - target[...].astype(F32)) / total).astype(BF16)
        q_out[...] = (dot_nt(d, w[...]) * scale[:, :1]).astype(BF16)
        grad[...] = dot_tn(a, d)

    low_logits, grad_second, q_low = call(
        low_second,
        "low_second",
        [shaped(rows, classes, F32), shaped(units, classes, F32), shaped(rows, units, BF16)],
        [adj, link_t, scale, w_second, low_target, h1_hub] + pieces2 + h1_mate,
    )

    q_mate = to_wide(q_low, 1)

    def back_first(
        adj_t, adj_t_mate, link, link_t, q, q_mate, grad_low, act_hub, agg_hub, q_hub, agg2_hub, dz_hub, *refs
    ):
        pieces, refs = refs[:n_own], refs[n_own:]
        turned, (keep, give) = refs[:n_own], refs[n_own:]
        q_own = q[...]
        around = jnp.concatenate([q_hub[...], q_hub[...]], axis=0)
        grad, at = None, 0
        for piece, agg in zip(pieces, turned):
            for n in range(0, piece.shape[0], rows):
                term = dot(adj_t[at : at + rows], q_own) + dot(adj_t_mate[at : at + rows], q_mate[...])
                if at == 0:
                    term = term + q_own.astype(F32) + dot(link_t[...], around)
                term = jnp.where(piece[n : n + rows].astype(F32) > 0.0, term, 0.0).astype(BF16)
                term = dot(agg[n : n + feat], term)
                grad = term if grad is None else grad + term
                at += rows
        sums = dot(link[:, :rows], q_own) + dot(link[:, rows:], q_own)
        mine = lax.broadcasted_iota(jnp.int32, (group, units), 0) < hr
        sums = sums + jnp.where(mine, q_hub[...].astype(F32), 0.0)
        sums = jnp.where(act_hub[...].astype(F32) > 0.0, sums, 0.0).astype(BF16)
        grad = grad + dot_tn(agg_hub[...], sums)
        grad_second = grad_low[...] + dot_tn(agg2_hub[...], dz_hub[...])
        core = lax.axis_index(WIDE) & 1

        @pl.when(core == 0)
        def _():
            keep[...] = grad
            give[...] = grad_second

        @pl.when(core == 1)
        def _():
            keep[...] = grad_second
            give[...] = grad

    keep, give = call(
        back_first,
        "back_first",
        [shaped(units, classes, F32), shaped(units, classes, F32)],
        [adj_t, adj_t_mate, link, link_t, q_low, q_mate, grad_second, h1_hub, agg1_hub, q_hub, agg2_hub, dz2_hub]
        + pieces2
        + turned,
    )
    got = to_wide(give, 1)

    n_share = 2 * n_hub
    share = units // n_share
    steps = [(2 * (k // n_hub), k % n_hub) for k in range(n_share)]

    def place_of():
        return ((lax.axis_index(WIDE) >> 1) & 1) * n_hub + lax.axis_index(HUB)

    def split(keep, got, *outs):
        me = place_of()
        for k, out in enumerate(outs):
            at = pl.ds(pl.multiple_of((me ^ k) * share, share), share)
            out[...] = keep[at] + got[at]

    shares = call(split, "split", [shaped(share, classes, F32) for _ in range(n_share)], [keep, got])
    shares = [to_both(shares[k], *steps[k]) for k in range(n_share - 1, 0, -1)] + [shares[0]]

    def add_up(*refs):
        refs[-1][...] = pairwise([r[...] for r in refs[:-1]])

    (mine,) = call(add_up, "add_xy", [shaped(share, classes, F32)], shares)
    parts = [to_wide(mine, 4 * k) for k in range(2, nz)] + [mine, to_wide(mine, 4)]
    (mine,) = call(add_up, "add_z", [shaped(share, classes, F32)], parts)
    mine = [to_both(mine, *steps[k]) for k in range(n_share - 1, 0, -1)] + [mine]
    other = [to_wide(m, 1) for m in mine]

    def assemble(*refs):
        mine, other, (grad_first, grad_second) = refs[:n_share], refs[n_share : 2 * n_share], refs[2 * n_share :]
        me = place_of()
        core = lax.axis_index(WIDE) & 1

        def write(mine_out, other_out):
            for k in range(n_share):
                at = pl.ds(pl.multiple_of((me ^ (n_share - 1 - k)) * share, share), share)
                mine_out[at] = mine[k][...]
                other_out[at] = other[k][...]

        @pl.when(core == 0)
        def _():
            write(grad_first, grad_second)

        @pl.when(core == 1)
        def _():
            write(grad_second, grad_first)

    grad_first, grad_second = call(
        assemble, "assemble", [shaped(units, classes, F32), shaped(units, classes, F32)], mine + other
    )
    return (low_logits, hub_logits, grad_first, grad_second)


def solution(mesh):
    in_specs = (
        P((WIDE, HUB), None),
        P((WIDE, HUB), None),
        P(),
        P(),
        P((WIDE, HUB), None, None),
        P((WIDE, HUB), None),
        P((WIDE, HUB)),
        P((WIDE, HUB)),
        P((WIDE, HUB)),
        P((WIDE, HUB)),
    )
    out_specs = (P((WIDE, HUB), None), P((WIDE, HUB), None), P(), P())
    return jax.shard_map(local, mesh=mesh, in_specs=in_specs, out_specs=out_specs, check_vma=False)
```

```python
import jax
import jax.numpy as jnp
from jax import lax
from jax.experimental import pallas as pl
from jax.experimental.pallas import tpu as pltpu
from jax.sharding import PartitionSpec as P

F32 = jnp.float32
BF16 = jnp.bfloat16
WIDE = "wide"
HUB = "hub"
LANES = 128
VMEM_BYTES = 16 * 1024 * 1024


def shaped(rows, cols, dtype):
    return jax.ShapeDtypeStruct((rows, cols), dtype)


def call(body, name, outs, ins, smem=(), traffic=1 << 20):
    spaces = [pltpu.SMEM if i in smem else pltpu.VMEM for i in range(len(ins))]
    return pl.pallas_call(
        body,
        name=name,
        out_shape=outs,
        in_specs=[pl.BlockSpec(memory_space=s) for s in spaces],
        out_specs=[pl.BlockSpec(memory_space=pltpu.VMEM) for _ in outs],
        cost_estimate=pl.CostEstimate(flops=0, bytes_accessed=traffic, transcendentals=0),
        compiler_params=pltpu.CompilerParams(vmem_limit_bytes=VMEM_BYTES),
    )(*ins)


def dot(a, b):
    return lax.dot_general(a, b, (((1,), (0,)), ((), ())), preferred_element_type=F32)


def dot_nt(a, b):
    return lax.dot_general(a, b, (((1,), (1,)), ((), ())), preferred_element_type=F32)


def dot_tn(a, b):
    return lax.dot_general(a, b, (((0,), (0,)), ((), ())), preferred_element_type=F32)


def to_wide(x, k):
    return lax.ppermute(x, WIDE, [(i, i ^ k) for i in range(lax.axis_size(WIDE))])


def to_both(x, k, j):
    n, m = lax.axis_size(WIDE), lax.axis_size(HUB)
    pairs = [(i * m + h, (i ^ k) * m + (h ^ j)) for i in range(n) for h in range(m)]
    return lax.ppermute(x, (WIDE, HUB), pairs)


def together(*values):
    return lax.optimization_barrier(values)


def join(*parts):
    def body(*refs):
        at = 0
        for ref in refs[:-1]:
            refs[-1][at : at + ref.shape[0]] = ref[...]
            at += ref.shape[0]

    (out,) = call(body, "join", [shaped(sum(p.shape[0] for p in parts), parts[0].shape[1], parts[0].dtype)], parts)
    return out


def direct(nz):
    return [3, 1] + list(range(4, nz))


def over_z(own):
    return [to_wide(own, 4 * k) for k in direct(lax.axis_size(WIDE) // 4)]


def onward(over_x, over_z, late=None):
    return [to_wide(over_x, 8), to_wide(over_z[0] if late is None else late, 4), to_wide(join(*over_z), 2)]


def place_of_block(z, x, nz):
    place = jnp.where(z == 2, nz + 1 - x, x)
    for at, k in enumerate(direct(nz), 2):
        place = jnp.where(z == k, at + x * nz, place)
    return place


def pairwise(parts):
    while len(parts) > 1:
        parts = [parts[i] + parts[i + 1] for i in range(0, len(parts), 2)]
    return parts[0]


def tile_sum(adj_ref, piece_refs):
    at, total = 0, None
    for ref in piece_refs:
        n = ref.shape[0]
        term = dot(adj_ref[:, at : at + n], ref[...])
        total = term if total is None else total + term
        at += n
    return total


def local(
    low_feats,
    hub_feats,
    w_first,
    w_second,
    low_tiles,
    tile_cols,
    edge_rows,
    edge_hubs,
    low_labels,
    hub_labels,
):
    rows, feat = low_feats.shape
    hr = hub_feats.shape[0]
    n_tiles, tile, _ = low_tiles.shape
    blocks = rows // tile
    per_block = n_tiles // blocks
    units = w_first.shape[1]
    classes = w_second.shape[1]
    n_wide, n_hub = lax.axis_size(WIDE), lax.axis_size(HUB)
    nz = n_wide // 4
    group = hr * n_hub
    total = (rows + hr) * n_wide * n_hub
    edges = edge_rows.shape[0]
    pay = feat + LANES
    half = n_wide * rows // 2

    feats_z, feats_x = over_z(low_feats), to_wide(low_feats, 2)

    mates = range(1, n_hub)

    def to_hub(x, k):
        return lax.ppermute(x, HUB, [(i, i ^ k) for i in range(n_hub)])

    at = [0]
    for n in (edges, edges, rows):
        at.append(at[-1] + n)
    ints = jnp.concatenate([edge_rows, edge_hubs, low_labels, hub_labels]).reshape(1, at[-1] + hr)

    def edge_tables(ints, feats, hub_rows, w, link, link_t, low_count, low_hot, feats_out, w_out, part):
        feats_out[...] = feats[...]
        w_out[...] = w[...]
        e_rows, e_hubs, labels = (ints[:, at[i] : at[i + 1]] for i in range(3))
        labels_hub = ints[:, at[3] :]
        h = lax.axis_index(HUB)
        hubs = ((e_hubs // hr) ^ h) * hr + e_hubs % hr
        row_hot = (lax.broadcasted_iota(jnp.int32, (rows, edges), 0) == e_rows).astype(BF16)
        hub_hot = (lax.broadcasted_iota(jnp.int32, (group, edges), 0) == hubs).astype(BF16)
        links = dot_nt(hub_hot, row_hot)
        links_t = dot_nt(row_hot, hub_hot)
        hi, hi_t = links.astype(BF16), links_t.astype(BF16)
        lo, lo_t = (links - hi.astype(F32)).astype(BF16), (links_t - hi_t.astype(F32)).astype(BF16)
        link[:, :rows] = hi
        link[:, rows:] = lo
        link_t[...] = jnp.concatenate([hi_t, lo_t], axis=1)
        low_count[...] = jnp.broadcast_to(jnp.sum(links_t, axis=1, keepdims=True), (rows, LANES))
        sums = dot(hi, feats[...]) + dot(lo, feats[...])
        counts = jnp.broadcast_to(jnp.sum(links, axis=1, keepdims=True), (group, LANES))
        part[:group, :feat] = sums
        part[:group, feat:] = counts
        part[group:, :feat] = hub_rows[...].astype(F32)
        part[group:, feat:] = jnp.broadcast_to(labels_hub.astype(F32), (LANES, hr)).T
        hot = (lax.broadcasted_iota(jnp.int32, (classes, rows), 0) == labels).astype(F32)
        low_hot[...] = hot.T.astype(BF16)

    link, link_t, low_count, low_target, near_feats, near_w, part1 = call(
        edge_tables,
        "edge_tables",
        [
            shaped(group, 2 * rows, BF16),
            shaped(rows, 2 * group, BF16),
            shaped(rows, LANES, F32),
            shaped(rows, classes, BF16),
            shaped(rows, feat, BF16),
            shaped(feat, units, BF16),
            shaped(group + hr, pay, F32),
        ],
        [ints, low_feats, hub_feats, w_first],
        traffic=4 << 20,
    )

    feats_z, feats_x, part1, low_count, near_feats, near_w = together(
        feats_z, feats_x, part1, low_count, near_feats, near_w
    )
    feats_on = onward(feats_x, feats_z)
    feats_mate = [to_wide(join(near_feats, feats_x, *feats_z), 1)]

    def adjacency(tiles, cols, low_count, adj, adj_t, adj_t_give, scale):
        w = lax.axis_index(WIDE)
        adj[...] = jnp.zeros_like(adj)
        adj_t[...] = jnp.zeros_like(adj_t)
        adj_t_give[...] = jnp.zeros_like(adj_t_give)
        for r in range(blocks):
            for k in range(per_block):
                b = cols[r, k]
                rel = (b // blocks) ^ w
                place = place_of_block(rel >> 2, (rel >> 1) & 1, nz)
                start = pl.multiple_of((place * blocks + b % blocks) * tile, tile)
                value = tiles[r * per_block + k]
                turned = value.T
                side = rel & 1
                at = pl.ds(pl.multiple_of(side * half + start, tile), tile)
                adj[r * tile : (r + 1) * tile, at] = value
                own = pl.multiple_of(jnp.where(side == 0, start, half), tile)
                give = pl.multiple_of(jnp.where(side == 1, start, half), tile)
                adj_t[pl.ds(own, tile), r * tile : (r + 1) * tile] = turned
                adj_t_give[pl.ds(give, tile), r * tile : (r + 1) * tile] = turned
        deg = dot(adj[...], jnp.ones((2 * half, LANES), BF16))
        scale[...] = lax.rsqrt(1.0 + deg + low_count[...])

    adj, adj_t, adj_t_give, scale = call(
        adjacency,
        "adjacency",
        [
            shaped(rows, 2 * half, BF16),
            shaped(half + tile, rows, BF16),
            shaped(half + tile, rows, BF16),
            shaped(rows, LANES, F32),
        ],
        [low_tiles, tile_cols, low_count],
        smem=(1,),
        traffic=14 << 20,
    )


    def group_sum(own, got):
        blocks = []
        for m in range(n_hub):
            block = own[m * hr : (m + 1) * hr]
            for k, g in enumerate(got, 1):
                block = block + g[(m ^ k) * hr : ((m ^ k) + 1) * hr]
            blocks.append(block)
        return jnp.concatenate(blocks, axis=0)

    def hub_first(w, own, *refs):
        got, (hub_scale, field, agg, act, target) = refs[:-5], refs[-5:]
        sums = group_sum(own, got)
        rest = jnp.concatenate([r[group:] for r in (own, *got)], axis=0)
        s = lax.rsqrt(1.0 + sums[:, feat : feat + 1])
        hub_scale[...] = jnp.broadcast_to(s, (group, LANES))
        field[...] = rest[:, :feat].astype(BF16)
        a = ((rest[:, :feat] + sums[:, :feat]) * s).astype(BF16)
        agg[...] = a
        act[...] = jnp.maximum(dot(a, w[...]), 0.0).astype(BF16)
        labels = rest[:, feat : feat + 1].astype(jnp.int32)
        target[...] = (lax.broadcasted_iota(jnp.int32, (group, classes), 1) == labels).astype(BF16)

    feats_on, scale, got1 = together(
        feats_on, scale, [to_hub(part1, k) for k in mates]
    )
    feats_mate.append(to_wide(join(*feats_on), 1))
    pieces1 = [near_feats, feats_x] + feats_z + feats_on + feats_mate
    hub_scale, hub_field, agg1_hub, h1_hub, hub_target = call(
        hub_first,
        "hub_first",
        [
            shaped(group, LANES, F32),
            shaped(group, feat, BF16),
            shaped(group, feat, BF16),
            shaped(group, units, BF16),
            shaped(group, classes, BF16),
        ],
        [near_w, part1] + got1,
    )

    def low_near(adj, link_t, around, *refs):
        pieces, out = refs[:-1], refs[-1]
        around = jnp.concatenate([around[...], around[...]], axis=0)
        out[...] = tile_sum(adj, pieces) + pieces[0][...].astype(F32) + dot(link_t[...], around)

    (sum_near,) = call(
        low_near, "low_near", [shaped(rows, feat, F32)], [adj, link_t, hub_field] + pieces1[:-1]
    )

    def low_first(adj, link, scale, w, sum_near, last, act_out, turned, sums):
        s = sum_near[...] + dot(adj[:, 2 * half - last.shape[0] :], last[...])
        a = (s * scale[:, :1]).astype(BF16)
        act = jnp.maximum(dot(a, w[...]), 0.0).astype(BF16)
        act_out[...] = act
        turned[...] = a.T
        sums[...] = dot(link[:, :rows], act) + dot(link[:, rows:], act)

    h1, agg1_t, part2 = call(
        low_first,
        "low_first",
        [shaped(rows, units, BF16), shaped(feat, rows, BF16), shaped(group, units, F32)],
        [adj, link, scale, near_w, sum_near, pieces1[-1]],
    )

    def hub_second(act, hub_scale, w, target, own, *refs):
        got, (logits, agg, dz, q) = refs[:-4], refs[-4:]
        s = hub_scale[:, :1]
        a = ((act[...].astype(F32) + group_sum(own, got)) * s).astype(BF16)
        y = dot(a, w[...])
        d = ((y - target[...].astype(F32)) / total).astype(BF16)
        agg[...] = a[:hr]
        logits[...] = y[:hr]
        dz[...] = d[:hr]
        q[...] = (dot_nt(d, w[...]) * s).astype(BF16)

    h1_z, h1_x = together(over_z(h1), to_wide(h1, 2))
    agg1_z, agg1_x, h1_z_late = together(over_z(agg1_t), to_wide(agg1_t, 2), h1_z[0])
    part2_late, _ = together(part2, agg1_x)
    got2 = [to_hub(part2_late, k) for k in mates]
    h1_on = onward(h1_x, h1_z, h1_z_late)
    h1_on, adj_t_give, got2 = together(h1_on, adj_t_give, got2)
    hub_logits, agg2_hub, dz2_hub, q_hub = call(
        hub_second,
        "hub_second",
        [shaped(hr, classes, F32), shaped(hr, units, BF16), shaped(hr, classes, BF16), shaped(group, units, BF16)],
        [h1_hub, hub_scale, w_second, hub_target, part2] + got2,
    )
    adj_t_mate = to_wide(adj_t_give, 1)
    agg1_on = onward(agg1_x, agg1_z)
    h1_mate = [to_wide(join(h1, h1_x, *h1_z, *h1_on), 1)]
    pieces2 = [h1, h1_x] + h1_z + h1_on
    turned = [agg1_t, agg1_x] + agg1_z + agg1_on
    n_own = len(pieces2)

    def low_second(adj, link_t, scale, w, target, act_hub, *refs):
        pieces, (logits, grad, q_out) = refs[: n_own + 1], refs[n_own + 1 :]
        around = jnp.concatenate([act_hub[...], act_hub[...]], axis=0)
        s = tile_sum(adj, pieces) + pieces[0][...].astype(F32) + dot(link_t[...], around)
        a = (s * scale[:, :1]).astype(BF16)
        y = dot(a, w[...])
        logits[...] = y
        d = ((y - target[...].astype(F32)) / total).astype(BF16)
        q_out[...] = (dot_nt(d, w[...]) * scale[:, :1]).astype(BF16)
        grad[...] = dot_tn(a, d)

    low_logits, grad_second, q_low = call(
        low_second,
        "low_second",
        [shaped(rows, classes, F32), shaped(units, classes, F32), shaped(rows, units, BF16)],
        [adj, link_t, scale, w_second, low_target, h1_hub] + pieces2 + h1_mate,
    )

    q_mate = to_wide(q_low, 1)

    def back_first(
        adj_t, adj_t_mate, link, link_t, q, q_mate, grad_low, act_hub, agg_hub, q_hub, agg2_hub, dz_hub, *refs
    ):
        pieces, refs = refs[:n_own], refs[n_own:]
        turned, (keep, give) = refs[:n_own], refs[n_own:]
        q_own = q[...]
        around = jnp.concatenate([q_hub[...], q_hub[...]], axis=0)
        grad, at = None, 0
        for piece, agg in zip(pieces, turned):
            for n in range(0, piece.shape[0], rows):
                term = dot(adj_t[at : at + rows], q_own) + dot(adj_t_mate[at : at + rows], q_mate[...])
                if at == 0:
                    term = term + q_own.astype(F32) + dot(link_t[...], around)
                term = jnp.where(piece[n : n + rows].astype(F32) > 0.0, term, 0.0).astype(BF16)
                term = dot(agg[n : n + feat], term)
                grad = term if grad is None else grad + term
                at += rows
        sums = dot(link[:, :rows], q_own) + dot(link[:, rows:], q_own)
        mine = lax.broadcasted_iota(jnp.int32, (group, units), 0) < hr
        sums = sums + jnp.where(mine, q_hub[...].astype(F32), 0.0)
        sums = jnp.where(act_hub[...].astype(F32) > 0.0, sums, 0.0).astype(BF16)
        grad = grad + dot_tn(agg_hub[...], sums)
        grad_second = grad_low[...] + dot_tn(agg2_hub[...], dz_hub[...])
        core = lax.axis_index(WIDE) & 1

        @pl.when(core == 0)
        def _():
            keep[...] = grad
            give[...] = grad_second

        @pl.when(core == 1)
        def _():
            keep[...] = grad_second
            give[...] = grad

    keep, give = call(
        back_first,
        "back_first",
        [shaped(units, classes, F32), shaped(units, classes, F32)],
        [adj_t, adj_t_mate, link, link_t, q_low, q_mate, grad_second, h1_hub, agg1_hub, q_hub, agg2_hub, dz2_hub]
        + pieces2
        + turned,
    )
    got = to_wide(give, 1)

    n_share = 2 * n_hub
    share = units // n_share
    steps = [(2 * (k // n_hub), k % n_hub) for k in range(n_share)]

    def place_of():
        return ((lax.axis_index(WIDE) >> 1) & 1) * n_hub + lax.axis_index(HUB)

    def split(keep, got, *outs):
        me = place_of()
        for k, out in enumerate(outs):
            at = pl.ds(pl.multiple_of((me ^ k) * share, share), share)
            out[...] = keep[at] + got[at]

    shares = call(split, "split", [shaped(share, classes, F32) for _ in range(n_share)], [keep, got])
    shares = [to_both(shares[k], *steps[k]) for k in range(n_share - 1, 0, -1)] + [shares[0]]

    def add_up(*refs):
        refs[-1][...] = pairwise([r[...] for r in refs[:-1]])

    (mine,) = call(add_up, "add_xy", [shaped(share, classes, F32)], shares)
    parts = [to_wide(mine, 4 * k) for k in range(2, nz)] + [mine, to_wide(mine, 4)]
    (mine,) = call(add_up, "add_z", [shaped(share, classes, F32)], parts)
    mine = [to_both(mine, *steps[k]) for k in range(n_share - 1, 0, -1)] + [mine]
    other = [to_wide(m, 1) for m in mine]

    def assemble(*refs):
        mine, other, (grad_first, grad_second) = refs[:n_share], refs[n_share : 2 * n_share], refs[2 * n_share :]
        me = place_of()
        core = lax.axis_index(WIDE) & 1

        def write(mine_out, other_out):
            for k in range(n_share):
                at = pl.ds(pl.multiple_of((me ^ (n_share - 1 - k)) * share, share), share)
                mine_out[at] = mine[k][...]
                other_out[at] = other[k][...]

        @pl.when(core == 0)
        def _():
            write(grad_first, grad_second)

        @pl.when(core == 1)
        def _():
            write(grad_second, grad_first)

    grad_first, grad_second = call(
        assemble, "assemble", [shaped(units, classes, F32), shaped(units, classes, F32)], mine + other
    )
    return (low_logits, hub_logits, grad_first, grad_second)


def solution(mesh):
    in_specs = (
        P((WIDE, HUB), None),
        P((WIDE, HUB), None),
        P(),
        P(),
        P((WIDE, HUB), None, None),
        P((WIDE, HUB), None),
        P((WIDE, HUB)),
        P((WIDE, HUB)),
        P((WIDE, HUB)),
        P((WIDE, HUB)),
    )
    out_specs = (P((WIDE, HUB), None), P((WIDE, HUB), None), P(), P())
    return jax.shard_map(local, mesh=mesh, in_specs=in_specs, out_specs=out_specs, check_vma=False)
```

```python
import jax
import jax.numpy as jnp
from jax import lax
from jax.experimental import pallas as pl
from jax.experimental.pallas import tpu as pltpu
from jax.sharding import PartitionSpec as P

F32 = jnp.float32
BF16 = jnp.bfloat16
WIDE = "wide"
HUB = "hub"
LANES = 128
VMEM_BYTES = 16 * 1024 * 1024


def shaped(rows, cols, dtype):
    return jax.ShapeDtypeStruct((rows, cols), dtype)


def call(body, name, outs, ins, smem=(), traffic=1 << 20):
    spaces = [pltpu.SMEM if i in smem else pltpu.VMEM for i in range(len(ins))]
    return pl.pallas_call(
        body,
        name=name,
        out_shape=outs,
        in_specs=[pl.BlockSpec(memory_space=s) for s in spaces],
        out_specs=[pl.BlockSpec(memory_space=pltpu.VMEM) for _ in outs],
        cost_estimate=pl.CostEstimate(flops=0, bytes_accessed=traffic, transcendentals=0),
        compiler_params=pltpu.CompilerParams(vmem_limit_bytes=VMEM_BYTES),
    )(*ins)


def dot(a, b):
    return lax.dot_general(a, b, (((1,), (0,)), ((), ())), preferred_element_type=F32)


def dot_nt(a, b):
    return lax.dot_general(a, b, (((1,), (1,)), ((), ())), preferred_element_type=F32)


def dot_tn(a, b):
    return lax.dot_general(a, b, (((0,), (0,)), ((), ())), preferred_element_type=F32)


def to_wide(x, k):
    return lax.ppermute(x, WIDE, [(i, i ^ k) for i in range(lax.axis_size(WIDE))])


def to_both(x, k, j):
    n, m = lax.axis_size(WIDE), lax.axis_size(HUB)
    pairs = [(i * m + h, (i ^ k) * m + (h ^ j)) for i in range(n) for h in range(m)]
    return lax.ppermute(x, (WIDE, HUB), pairs)


def together(*values):
    return lax.optimization_barrier(values)


def join(*parts):
    def body(*refs):
        at = 0
        for ref in refs[:-1]:
            refs[-1][at : at + ref.shape[0]] = ref[...]
            at += ref.shape[0]

    (out,) = call(body, "join", [shaped(sum(p.shape[0] for p in parts), parts[0].shape[1], parts[0].dtype)], parts)
    return out


def direct(nz):
    return [3, 1] + list(range(4, nz))


def over_z(own):
    return [to_wide(own, 4 * k) for k in direct(lax.axis_size(WIDE) // 4)]


def onward(over_x, over_z, late=None):
    return [to_wide(over_x, 8), to_wide(over_z[0] if late is None else late, 4), to_wide(join(*over_z), 2)]


def place_of_block(z, x, nz):
    place = jnp.where(z == 2, nz + 1 - x, x)
    for at, k in enumerate(direct(nz), 2):
        place = jnp.where(z == k, at + x * nz, place)
    return place


def pairwise(parts):
    while len(parts) > 1:
        parts = [parts[i] + parts[i + 1] for i in range(0, len(parts), 2)]
    return parts[0]


def tile_sum(adj_ref, piece_refs):
    at, total = 0, None
    for ref in piece_refs:
        n = ref.shape[0]
        term = dot(adj_ref[:, at : at + n], ref[...])
        total = term if total is None else total + term
        at += n
    return total


def local(
    low_feats,
    hub_feats,
    w_first,
    w_second,
    low_tiles,
    tile_cols,
    edge_rows,
    edge_hubs,
    low_labels,
    hub_labels,
):
    rows, feat = low_feats.shape
    hr = hub_feats.shape[0]
    n_tiles, tile, _ = low_tiles.shape
    blocks = rows // tile
    per_block = n_tiles // blocks
    units = w_first.shape[1]
    classes = w_second.shape[1]
    n_wide, n_hub = lax.axis_size(WIDE), lax.axis_size(HUB)
    nz = n_wide // 4
    group = hr * n_hub
    total = (rows + hr) * n_wide * n_hub
    edges = edge_rows.shape[0]
    pay = feat + LANES
    half = n_wide * rows // 2

    feats_z, feats_x = over_z(low_feats), to_wide(low_feats, 2)

    mates = range(1, n_hub)

    def to_hub(x, k):
        return lax.ppermute(x, HUB, [(i, i ^ k) for i in range(n_hub)])

    at = [0]
    for n in (edges, edges, rows):
        at.append(at[-1] + n)
    ints = jnp.concatenate([edge_rows, edge_hubs, low_labels, hub_labels]).reshape(1, at[-1] + hr)

    def edge_tables(ints, feats, hub_rows, w, link, link_t, low_count, low_hot, feats_out, w_out, part):
        feats_out[...] = feats[...]
        w_out[...] = w[...]
        e_rows, e_hubs, labels = (ints[:, at[i] : at[i + 1]] for i in range(3))
        labels_hub = ints[:, at[3] :]
        h = lax.axis_index(HUB)
        hubs = ((e_hubs // hr) ^ h) * hr + e_hubs % hr
        row_hot = (lax.broadcasted_iota(jnp.int32, (rows, edges), 0) == e_rows).astype(BF16)
        hub_hot = (lax.broadcasted_iota(jnp.int32, (group, edges), 0) == hubs).astype(BF16)
        links = dot_nt(hub_hot, row_hot)
        links_t = dot_nt(row_hot, hub_hot)
        hi, hi_t = links.astype(BF16), links_t.astype(BF16)
        lo, lo_t = (links - hi.astype(F32)).astype(BF16), (links_t - hi_t.astype(F32)).astype(BF16)
        link[:, :rows] = hi
        link[:, rows:] = lo
        link_t[...] = jnp.concatenate([hi_t, lo_t], axis=1)
        low_count[...] = jnp.broadcast_to(jnp.sum(links_t, axis=1, keepdims=True), (rows, LANES))
        sums = dot(hi, feats[...]) + dot(lo, feats[...])
        counts = jnp.broadcast_to(jnp.sum(links, axis=1, keepdims=True), (group, LANES))
        part[:group, :feat] = sums
        part[:group, feat:] = counts
        part[group:, :feat] = hub_rows[...].astype(F32)
        part[group:, feat:] = jnp.broadcast_to(labels_hub.astype(F32), (LANES, hr)).T
        hot = (lax.broadcasted_iota(jnp.int32, (classes, rows), 0) == labels).astype(F32)
        low_hot[...] = hot.T.astype(BF16)

    link, link_t, low_count, low_target, near_feats, near_w, part1 = call(
        edge_tables,
        "edge_tables",
        [
            shaped(group, 2 * rows, BF16),
            shaped(rows, 2 * group, BF16),
            shaped(rows, LANES, F32),
            shaped(rows, classes, BF16),
            shaped(rows, feat, BF16),
            shaped(feat, units, BF16),
            shaped(group + hr, pay, F32),
        ],
        [ints, low_feats, hub_feats, w_first],
        traffic=4 << 20,
    )

    feats_z, feats_x, part1, low_count, near_feats, near_w = together(
        feats_z, feats_x, part1, low_count, near_feats, near_w
    )
    feats_on = onward(feats_x, feats_z)
    feats_mate = [to_wide(join(near_feats, feats_x, *feats_z), 1)]

    def adjacency(tiles, cols, low_count, adj, adj_t, adj_t_give, scale):
        w = lax.axis_index(WIDE)
        adj[...] = jnp.zeros_like(adj)
        adj_t[...] = jnp.zeros_like(adj_t)
        adj_t_give[...] = jnp.zeros_like(adj_t_give)
        for r in range(blocks):
            for k in range(per_block):
                b = cols[r, k]
                rel = (b // blocks) ^ w
                place = place_of_block(rel >> 2, (rel >> 1) & 1, nz)
                start = pl.multiple_of((place * blocks + b % blocks) * tile, tile)
                value = tiles[r * per_block + k]
                turned = value.T
                side = rel & 1
                at = pl.ds(pl.multiple_of(side * half + start, tile), tile)
                adj[r * tile : (r + 1) * tile, at] = value
                own = pl.multiple_of(jnp.where(side == 0, start, half), tile)
                give = pl.multiple_of(jnp.where(side == 1, start, half), tile)
                adj_t[pl.ds(own, tile), r * tile : (r + 1) * tile] = turned
                adj_t_give[pl.ds(give, tile), r * tile : (r + 1) * tile] = turned
        deg = dot(adj[...], jnp.ones((2 * half, LANES), BF16))
        scale[...] = lax.rsqrt(1.0 + deg + low_count[...])

    adj, adj_t, adj_t_give, scale = call(
        adjacency,
        "adjacency",
        [
            shaped(rows, 2 * half, BF16),
            shaped(half + tile, rows, BF16),
            shaped(half + tile, rows, BF16),
            shaped(rows, LANES, F32),
        ],
        [low_tiles, tile_cols, low_count],
        smem=(1,),
        traffic=14 << 20,
    )


    def group_sum(own, got):
        blocks = []
        for m in range(n_hub):
            block = own[m * hr : (m + 1) * hr]
            for k, g in enumerate(got, 1):
                block = block + g[(m ^ k) * hr : ((m ^ k) + 1) * hr]
            blocks.append(block)
        return jnp.concatenate(blocks, axis=0)

    def hub_first(w, own, *refs):
        got, (hub_scale, field, agg, act, target) = refs[:-5], refs[-5:]
        sums = group_sum(own, got)
        rest = jnp.concatenate([r[group:] for r in (own, *got)], axis=0)
        s = lax.rsqrt(1.0 + sums[:, feat : feat + 1])
        hub_scale[...] = jnp.broadcast_to(s, (group, LANES))
        field[...] = rest[:, :feat].astype(BF16)
        a = ((rest[:, :feat] + sums[:, :feat]) * s).astype(BF16)
        agg[...] = a
        act[...] = jnp.maximum(dot(a, w[...]), 0.0).astype(BF16)
        labels = rest[:, feat : feat + 1].astype(jnp.int32)
        target[...] = (lax.broadcasted_iota(jnp.int32, (group, classes), 1) == labels).astype(BF16)

    feats_on, scale, got1 = together(
        feats_on, scale, [to_hub(part1, k) for k in mates]
    )
    feats_mate.append(to_wide(join(*feats_on), 1))
    pieces1 = [near_feats, feats_x] + feats_z + feats_on + feats_mate
    hub_scale, hub_field, agg1_hub, h1_hub, hub_target = call(
        hub_first,
        "hub_first",
        [
            shaped(group, LANES, F32),
            shaped(group, feat, BF16),
            shaped(group, feat, BF16),
            shaped(group, units, BF16),
            shaped(group, classes, BF16),
        ],
        [near_w, part1] + got1,
    )

    def low_near(adj, link_t, around, *refs):
        pieces, out = refs[:-1], refs[-1]
        around = jnp.concatenate([around[...], around[...]], axis=0)
        out[...] = tile_sum(adj, pieces) + pieces[0][...].astype(F32) + dot(link_t[...], around)

    (sum_near,) = call(
        low_near, "low_near", [shaped(rows, feat, F32)], [adj, link_t, hub_field] + pieces1[:-1]
    )

    def low_first(adj, link, scale, w, sum_near, last, act_out, turned, sums):
        s = sum_near[...] + dot(adj[:, 2 * half - last.shape[0] :], last[...])
        a = (s * scale[:, :1]).astype(BF16)
        act = jnp.maximum(dot(a, w[...]), 0.0).astype(BF16)
        act_out[...] = act
        turned[...] = a.T
        sums[...] = dot(link[:, :rows], act) + dot(link[:, rows:], act)

    h1, agg1_t, part2 = call(
        low_first,
        "low_first",
        [shaped(rows, units, BF16), shaped(feat, rows, BF16), shaped(group, units, F32)],
        [adj, link, scale, near_w, sum_near, pieces1[-1]],
    )

    def hub_second(act, hub_scale, w, target, own, *refs):
        got, (logits, agg, dz, q) = refs[:-4], refs[-4:]
        s = hub_scale[:, :1]
        a = ((act[...].astype(F32) + group_sum(own, got)) * s).astype(BF16)
        y = dot(a, w[...])
        d = ((y - target[...].astype(F32)) / total).astype(BF16)
        agg[...] = a[:hr]
        logits[...] = y[:hr]
        dz[...] = d[:hr]
        q[...] = (dot_nt(d, w[...]) * s).astype(BF16)

    h1_z, h1_x = together(over_z(h1), to_wide(h1, 2))
    agg1_z, agg1_x, h1_z_late = together(over_z(agg1_t), to_wide(agg1_t, 2), h1_z[0])
    part2_late, _ = together(part2, agg1_x)
    got2 = [to_hub(part2_late, k) for k in mates]
    h1_on = onward(h1_x, h1_z, h1_z_late)
    h1_on, adj_t_give, got2 = together(h1_on, adj_t_give, got2)
    hub_logits, agg2_hub, dz2_hub, q_hub = call(
        hub_second,
        "hub_second",
        [shaped(hr, classes, F32), shaped(hr, units, BF16), shaped(hr, classes, BF16), shaped(group, units, BF16)],
        [h1_hub, hub_scale, w_second, hub_target, part2] + got2,
    )
    adj_t_mate = to_wide(adj_t_give, 1)
    agg1_on = onward(agg1_x, agg1_z)
    h1_mate = [to_wide(join(h1, h1_x, *h1_z, *h1_on), 1)]
    pieces2 = [h1, h1_x] + h1_z + h1_on
    turned = [agg1_t, agg1_x] + agg1_z + agg1_on
    n_own = len(pieces2)

    def low_second(adj, link_t, scale, w, target, act_hub, *refs):
        pieces, (logits, grad, q_out) = refs[: n_own + 1], refs[n_own + 1 :]
        around = jnp.concatenate([act_hub[...], act_hub[...]], axis=0)
        s = tile_sum(adj, pieces) + pieces[0][...].astype(F32) + dot(link_t[...], around)
        a = (s * scale[:, :1]).astype(BF16)
        y = dot(a, w[...])
        logits[...] = y
        d = ((y - target[...].astype(F32)) / total).astype(BF16)
        q_out[...] = (dot_nt(d, w[...]) * scale[:, :1]).astype(BF16)
        grad[...] = dot_tn(a, d)

    low_logits, grad_second, q_low = call(
        low_second,
        "low_second",
        [shaped(rows, classes, F32), shaped(units, classes, F32), shaped(rows, units, BF16)],
        [adj, link_t, scale, w_second, low_target, h1_hub] + pieces2 + h1_mate,
    )

    q_mate = to_wide(q_low, 1)

    def back_first(
        adj_t, adj_t_mate, link, link_t, q, q_mate, grad_low, act_hub, agg_hub, q_hub, agg2_hub, dz_hub, *refs
    ):
        pieces, refs = refs[:n_own], refs[n_own:]
        turned, (keep, give) = refs[:n_own], refs[n_own:]
        q_own = q[...]
        around = jnp.concatenate([q_hub[...], q_hub[...]], axis=0)
        grad, at = None, 0
        for piece, agg in zip(pieces, turned):
            for n in range(0, piece.shape[0], rows):
                term = dot(adj_t[at : at + rows], q_own) + dot(adj_t_mate[at : at + rows], q_mate[...])
                if at == 0:
                    term = term + q_own.astype(F32) + dot(link_t[...], around)
                term = jnp.where(piece[n : n + rows].astype(F32) > 0.0, term, 0.0).astype(BF16)
                term = dot(agg[n : n + feat], term)
                grad = term if grad is None else grad + term
                at += rows
        sums = dot(link[:, :rows], q_own) + dot(link[:, rows:], q_own)
        mine = lax.broadcasted_iota(jnp.int32, (group, units), 0) < hr
        sums = sums + jnp.where(mine, q_hub[...].astype(F32), 0.0)
        sums = jnp.where(act_hub[...].astype(F32) > 0.0, sums, 0.0).astype(BF16)
        grad = grad + dot_tn(agg_hub[...], sums)
        grad_second = grad_low[...] + dot_tn(agg2_hub[...], dz_hub[...])
        core = lax.axis_index(WIDE) & 1

        @pl.when(core == 0)
        def _():
            keep[...] = grad
            give[...] = grad_second

        @pl.when(core == 1)
        def _():
            keep[...] = grad_second
            give[...] = grad

    keep, give = call(
        back_first,
        "back_first",
        [shaped(units, classes, F32), shaped(units, classes, F32)],
        [adj_t, adj_t_mate, link, link_t, q_low, q_mate, grad_second, h1_hub, agg1_hub, q_hub, agg2_hub, dz2_hub]
        + pieces2
        + turned,
    )
    got = to_wide(give, 1)

    n_share = 2 * n_hub
    share = units // n_share
    steps = [(2 * (k // n_hub), k % n_hub) for k in range(n_share)]

    def place_of():
        return ((lax.axis_index(WIDE) >> 1) & 1) * n_hub + lax.axis_index(HUB)

    def split(keep, got, *outs):
        me = place_of()
        for k, out in enumerate(outs):
            at = pl.ds(pl.multiple_of((me ^ k) * share, share), share)
            out[...] = keep[at] + got[at]

    shares = call(split, "split", [shaped(share, classes, F32) for _ in range(n_share)], [keep, got])
    turn = [n_share - 1] + list(range(1, n_share - 1))
    shares = [to_both(shares[k], *steps[k]) for k in turn] + [shares[0]]

    def add_up(*refs):
        refs[-1][...] = pairwise([r[...] for r in refs[:-1]])

    (mine,) = call(add_up, "add_xy", [shaped(share, classes, F32)], shares)
    parts = [to_wide(mine, 4 * k) for k in range(2, nz)] + [mine, to_wide(mine, 4)]
    (mine,) = call(add_up, "add_z", [shaped(share, classes, F32)], parts)
    mine = [to_both(mine, *steps[k]) for k in range(n_share - 1, 0, -1)] + [mine]
    other = [to_wide(m, 1) for m in mine]

    def assemble(*refs):
        mine, other, (grad_first, grad_second) = refs[:n_share], refs[n_share : 2 * n_share], refs[2 * n_share :]
        me = place_of()
        core = lax.axis_index(WIDE) & 1

        def write(mine_out, other_out):
            for k in range(n_share):
                at = pl.ds(pl.multiple_of((me ^ (n_share - 1 - k)) * share, share), share)
                mine_out[at] = mine[k][...]
                other_out[at] = other[k][...]

        @pl.when(core == 0)
        def _():
            write(grad_first, grad_second)

        @pl.when(core == 1)
        def _():
            write(grad_second, grad_first)

    grad_first, grad_second = call(
        assemble, "assemble", [shaped(units, classes, F32), shaped(units, classes, F32)], mine + other
    )
    return (low_logits, hub_logits, grad_first, grad_second)


def solution(mesh):
    in_specs = (
        P((WIDE, HUB), None),
        P((WIDE, HUB), None),
        P(),
        P(),
        P((WIDE, HUB), None, None),
        P((WIDE, HUB), None),
        P((WIDE, HUB)),
        P((WIDE, HUB)),
        P((WIDE, HUB)),
        P((WIDE, HUB)),
    )
    out_specs = (P((WIDE, HUB), None), P((WIDE, HUB), None), P(), P())
    return jax.shard_map(local, mesh=mesh, in_specs=in_specs, out_specs=out_specs, check_vma=False)
```
